32 devices in a mesh: member: 2 (over x), tile: 16 (over z, y, core).
Axes of the slice: x: 2, y: 2, z: 4, core: 2. Of those that a mesh axis runs over, the one named last changes fastest.
Arguments:
- inputs: bfloat16 [2, 8192, 512], P('member', 'tile'), may hold values from -6 to 6
- noise: bfloat16 [2, 8192, 128], P('member', 'tile'), may hold values from -6 to 6
- neighbours: int32 [8, 8192], P(None, 'tile'), may hold values from 0 to 639, as said below
- region_map: int32 [16], P('tile'), may hold values from 0 to 7, as said below
- msg_weight: bfloat16 [512, 512], replicated, may hold values from -0.25 to 0.25
- up_weight: bfloat16 [512, 1024], replicated, may hold values from -0.25 to 0.25
- down_weight: bfloat16 [1024, 512], replicated, may hold values from -0.1875 to 0.1875
- student_in: bfloat16 [512, 512], replicated, may hold values from -0.25 to 0.25
- student_noise: bfloat16 [128, 512], replicated, may hold values from -0.5 to 0.5
- student_out: bfloat16 [512, 512], replicated, may hold values from -0.25 to 0.25
Outputs:
- teacher_out: bfloat16 [2, 8192, 512], P('member', 'tile')
- region_loss: float32 [8], replicated
- grad_in: float32 [512, 512], P('tile')
- grad_noise: float32 [128, 512], P('tile')
- grad_out: float32 [512, 512], P('tile')
The draws below stay inside these ranges and needn't reach their ends.
Inputs may be any that keep to these rules, and one draw needn't show every extreme that they name: `neighbours`: each index lies within 64 of the cell's own row (its row plus 64); the first index of a tile's first cell is 0 and that of its last cell is 639. `region_map`: each region holds 2 tiles.
All inputs are finite; a program needn't handle non-finite values.
Results may differ from the reference program's by a relative error of at most 0.0039.
The reference program's roundings to bfloat16 on the way (of `gathered`, `normed`, `hidden`, `shidden`, `student`, `gstudent` and `gpre`) count: a program that leaves them out, or rounds other values in their place, can miss the bound.
Values may be sent and summed in bfloat16 or wider, within the bound.
A program may use at most 64 MiB of HBM per device.

```python
import math
import jax
import jax.numpy as jnp
from jax import lax

D = 512
FF = 1024
H = 512
NOISE = 128
NBRS = 8
HALO = 64
REGIONS = 8
CELLS = 512
MEMBERS = 2
TILES = 16
CELLS_ALL = 8192


def draw_neighbours(key, part):
    offsets = jax.random.randint(key, (NBRS, CELLS_ALL), -HALO, HALO + 1).astype(jnp.int32)
    local = jnp.arange(CELLS_ALL, dtype=jnp.int32) % CELLS
    indices = local[None, :] + HALO + offsets
    first_row = jnp.where(local == 0, 0, jnp.where(local == CELLS - 1, CELLS + 2 * HALO - 1, indices[0]))
    return indices.at[0].set(first_row).astype(jnp.int32)


def draw_region_map(key, part):
    order = jax.random.permutation(key, TILES)
    return (order % REGIONS).astype(jnp.int32)


def steps_of(rng, shape, pieces, low, high):
    level = 1.0
    for axis_at, shards_of in pieces:
        heights = jax.random.uniform(jax.random.fold_in(jax.random.fold_in(rng, 6), axis_at), (shards_of,), jnp.float32, low / len(pieces), high / len(pieces))
        level = level * jnp.repeat(jnp.exp(heights), shape[axis_at] // shards_of).reshape((-1,) + (1,) * (len(shape) - 1 - axis_at))
    return level


def bell_draw(own_key, dims, deviation, most, cuts=(), held_as=jnp.bfloat16):
    loudness = steps_of(own_key, dims, cuts, -0.22, 0.18) if cuts else 1.0
    drawn = jax.random.normal(own_key, dims, jnp.float32) * deviation * loudness
    return jnp.minimum(jnp.maximum(drawn, -most), most).astype(held_as)


def setup_inputs(seed: int = 0) -> dict:
    splits = jax.random.split(jax.random.key(seed), 11)
    inputs = bell_draw(splits[0], (MEMBERS, CELLS_ALL, D), 1.0, 6.0, ((0, 2), (1, 16)))
    noise = bell_draw(splits[1], (MEMBERS, CELLS_ALL, NOISE), 1.0, 6.0, ((0, 2), (1, 16)))
    neighbours = draw_neighbours(jax.random.fold_in(splits[10], 71), 0)
    region_map = draw_region_map(jax.random.fold_in(splits[10], 71), 0)
    msg_weight = bell_draw(splits[4], (D, D), D ** -0.5, 0.25)
    up_weight = bell_draw(splits[5], (D, FF), D ** -0.5, 0.25)
    down_weight = bell_draw(splits[6], (FF, D), FF ** -0.5, 0.1875)
    student_in = bell_draw(splits[7], (D, H), D ** -0.5, 0.25)
    student_noise = bell_draw(splits[8], (NOISE, H), NOISE ** -0.5, 0.5)
    student_out = bell_draw(splits[9], (H, D), H ** -0.5, 0.25)
    return dict(inputs=inputs, noise=noise, neighbours=neighbours, region_map=region_map, msg_weight=msg_weight, up_weight=up_weight, down_weight=down_weight, student_in=student_in, student_noise=student_noise, student_out=student_out)


def smooth(diff):
    return jnp.sqrt(diff * diff + 0.01) - 0.1

def smooth_grad(diff):
    return diff / jnp.sqrt(diff * diff + 0.01)

def silu_grad(value):
    sig = jax.nn.sigmoid(value)
    return sig * (1.0 + value * (1.0 - sig))

def reference(inputs, noise, neighbours, region_map, msg_weight, up_weight, down_weight, student_in, student_noise, student_out):
    members = MEMBERS
    cell_ids = jnp.arange(CELLS_ALL, dtype=jnp.int32)
    cell_tile = cell_ids // CELLS
    padded_ids = (cell_tile[None, :] * CELLS + neighbours).astype(jnp.int32)

    def teacher(state):
        padded = jnp.pad(state, ((HALO, HALO), (0, 0)))
        total = jnp.zeros((CELLS_ALL, D), jnp.float32)
        for column in range(NBRS):
            total = total + padded[padded_ids[column]].astype(jnp.float32)
        gathered = (total / NBRS).astype(jnp.bfloat16)
        resid = state.astype(jnp.float32) + jnp.dot(gathered, msg_weight, preferred_element_type=jnp.float32)
        normed = (resid * lax.rsqrt(lax.optimization_barrier(jnp.mean(resid * resid, axis=1, keepdims=True)) + 1e-06)).astype(jnp.bfloat16)
        hidden = jax.nn.silu(jnp.dot(normed, up_weight, preferred_element_type=jnp.float32)).astype(jnp.bfloat16)
        return (resid + jnp.dot(hidden, down_weight, preferred_element_type=jnp.float32)).astype(jnp.bfloat16)
    teacher_out = lax.map(teacher, inputs)

    def forward(pair):
        state, draws = pair
        preact = jnp.dot(state, student_in, preferred_element_type=jnp.float32) + jnp.dot(draws, student_noise, preferred_element_type=jnp.float32)
        shidden = jax.nn.silu(preact).astype(jnp.bfloat16)
        return (state.astype(jnp.float32) + jnp.dot(shidden, student_out, preferred_element_type=jnp.float32)).astype(jnp.bfloat16)
    student = lax.map(forward, (inputs, noise))
    s_all = student.astype(jnp.float32)
    t_all = teacher_out.astype(jnp.float32)

    def visit(carry, other):
        grads, losses = carry
        other_s, other_t = other
        cross = s_all - other_t[None]
        within = s_all - other_s[None]
        grads = grads + smooth_grad(cross) / (members * members) - smooth_grad(within) / (members * (members - 1))
        losses = losses + lax.optimization_barrier(jnp.sum(smooth(cross) / (members * members) - smooth(within) / (2 * members * (members - 1)), axis=(0, 2)))
        return ((grads, losses), None)
    start = (jnp.zeros_like(s_all), jnp.zeros((CELLS_ALL,), jnp.float32))
    (grads, crps), _ = lax.scan(visit, start, (s_all, t_all))
    gstudent = (grads * (1.0 / math.sqrt(CELLS_ALL))).astype(jnp.bfloat16)
    tile_sums = lax.optimization_barrier(jnp.sum(crps.reshape(TILES, CELLS), axis=1))
    onehot = (region_map[:, None] == jnp.arange(REGIONS, dtype=jnp.int32)[None, :]).astype(jnp.float32)
    region_loss = lax.optimization_barrier(jnp.sum(onehot * tile_sums[:, None], axis=0)) / (CELLS_ALL // REGIONS * D)

    def backward(carry, item):
        acc_in, acc_noise, acc_out = carry
        state, draws, gmember = item
        preact = jnp.dot(state, student_in, preferred_element_type=jnp.float32) + jnp.dot(draws, student_noise, preferred_element_type=jnp.float32)
        shidden = jax.nn.silu(preact).astype(jnp.bfloat16)
        acc_out = acc_out + jnp.dot(shidden.T, gmember, preferred_element_type=jnp.float32)
        gpre = (jnp.dot(gmember, student_out.T, preferred_element_type=jnp.float32) * silu_grad(preact)).astype(jnp.bfloat16)
        acc_in = acc_in + jnp.dot(state.T, gpre, preferred_element_type=jnp.float32)
        acc_noise = acc_noise + jnp.dot(draws.T, gpre, preferred_element_type=jnp.float32)
        return ((acc_in, acc_noise, acc_out), None)
    zeros = (jnp.zeros((D, H), jnp.float32), jnp.zeros((NOISE, H), jnp.float32), jnp.zeros((H, D), jnp.float32))
    (grad_in, grad_noise, grad_out), _ = lax.scan(backward, zeros, (inputs, noise, gstudent))
    return (teacher_out, region_loss, grad_in, grad_noise, grad_out)
```

```python
import functools
import math

import jax
import jax.numpy as jnp
from jax import lax
from jax.experimental import pallas as pl
from jax.experimental.pallas import tpu as pltpu
from jax.sharding import PartitionSpec as P

HALO = 64
REGIONS = 8
MESH = pl.DeviceIdType.MESH
F32 = jnp.float32
BF16 = jnp.bfloat16


def dot(a, b):
    return jnp.dot(a, b, preferred_element_type=F32)


def dot_tn(a, b):
    return lax.dot_general(a, b, (((0,), (0,)), ((), ())), preferred_element_type=F32)


def dot_nt(a, b):
    return lax.dot_general(a, b, (((1,), (1,)), ((), ())), preferred_element_type=F32)


def tile_digits(tiles):
    digits = []
    stride = 1
    for _ in range(2):
        if tiles // stride % 2 == 0 and tiles // stride > 2:
            digits.append((stride, 2))
            stride *= 2
    digits.append((stride, tiles // stride))
    return digits


def orders(tiles):
    digits = tile_digits(tiles)
    first = [digits[0], "member"] + digits[1:]
    second = digits[:2] + ["member"] + digits[2:]
    return first, second


def count_of(step, members):
    return members if step == "member" else step[1]


def slot_of(order, members, member, tile):
    slot = 0
    for step in order:
        n = count_of(step, members)
        slot = slot * n + (member if step == "member" else tile // step[0] % n)
    return slot


def layout(members, tiles):
    names = ["left", "right"]
    for o in range(1, members):
        names += [("state", o), ("noise", o), ("teacher", o)]
    for s, order in enumerate(orders(tiles)):
        for k, step in enumerate(order):
            for o in range(1, count_of(step, members)):
                names.append(("grad", s, k, o))
                if s == 0:
                    names.append(("loss", k, o))
        for o in range(1, members):
            names.append(("share", s, o))
    return {name: i for i, name in enumerate(names)}


def kernel(
    members,
    tiles,
    reduce_here,
    state_ref,
    noise_ref,
    neigh_ref,
    region_ref,
    msg_ref,
    up_ref,
    down_ref,
    sin_ref,
    snoise_ref,
    sout_ref,
    teacher_ref,
    loss_ref,
    gin_ref,
    gnoise_ref,
    gout_ref,
    ext,
    gathered,
    x_all,
    n_all,
    t_all,
    s_all,
    pre_all,
    sh_all,
    g_all,
    send_sem,
    recv_sem,
    *bufs,
):
    cells, width = state_ref.shape
    block = cells // members
    m = lax.axis_index("member")
    t = lax.axis_index("tile")
    ids = layout(members, tiles)
    streams = orders(tiles)

    def peer(step, o):
        if step == "member":
            other = lax.rem(m + o, members)
            return (other, t), other
        stride, n = step
        digit = lax.rem(t // stride, n)
        other = lax.rem(digit + o, n)
        return (m, t + (other - digit) * stride), other

    def digit_of(step):
        return m if step == "member" else lax.rem(t // step[0], step[1])

    def copy(name, src, dst, device):
        i = ids[name]
        return pltpu.make_async_remote_copy(
            src_ref=src,
            dst_ref=dst,
            send_sem=send_sem.at[i],
            recv_sem=recv_sem.at[i],
            device_id=device,
            device_id_type=MESH,
        )

    barrier = pltpu.get_barrier_semaphore()
    groups = ["member"] + (tile_digits(tiles) if reduce_here else [])
    waits = 0
    for step in groups:
        for o in range(1, count_of(step, members)):
            device, _ = peer(step, o)
            pl.semaphore_signal(barrier, inc=1, device_id=device, device_id_type=MESH)
            waits += 1

    @pl.when(t > 0)
    def _():
        pl.semaphore_signal(barrier, inc=1, device_id=(m, t - 1), device_id_type=MESH)

    @pl.when(t < tiles - 1)
    def _():
        pl.semaphore_signal(barrier, inc=1, device_id=(m, t + 1), device_id_type=MESH)

    ends = jnp.where(t > 0, 1, 0) + jnp.where(t < tiles - 1, 1, 0)
    pl.semaphore_wait(barrier, waits + ends)

    to_left = copy("left", state_ref.at[pl.ds(0, HALO)], ext.at[pl.ds(HALO + cells, HALO)], (m, t - 1))
    to_right = copy("right", state_ref.at[pl.ds(cells - HALO, HALO)], ext.at[pl.ds(0, HALO)], (m, t + 1))

    @pl.when(t > 0)
    def _():
        to_left.start()

    @pl.when(t < tiles - 1)
    def _():
        to_right.start()

    pending = []
    sent = {}
    for o in range(1, members):
        device, other = peer("member", o)
        rows = pl.ds(pl.multiple_of(other * block, block), block)
        slot = pl.ds(o * block, block)
        sent["state", o] = copy(("state", o), state_ref.at[rows], x_all.at[slot], device)
        sent["noise", o] = copy(("noise", o), noise_ref.at[rows], n_all.at[slot], device)
        sent["state", o].start()
        sent["noise", o].start()
        sent["teacher", o] = copy(("teacher", o), teacher_ref.at[rows], t_all.at[slot], device)

    own = pl.ds(pl.multiple_of(m * block, block), block)
    x_all[pl.ds(0, block)] = state_ref[own, :]
    n_all[pl.ds(0, block)] = noise_ref[own, :]
    ext[pl.ds(HALO, cells)] = state_ref[...]

    def student(o):
        rows = pl.ds(o * block, block)
        x = x_all[rows, :]
        pre = dot(x, sin_ref[...]) + dot(n_all[rows, :], snoise_ref[...])
        pre_all[rows, :] = pre
        sh = (pre * jax.nn.sigmoid(pre)).astype(BF16)
        sh_all[rows, :] = sh
        s_all[rows, :] = (x.astype(F32) + dot(sh, sout_ref[...])).astype(BF16)

    student(0)

    zeros = jnp.zeros((HALO, width), BF16)

    @pl.when(t > 0)
    def _():
        to_right.wait_recv()

    @pl.when(t == 0)
    def _():
        ext[pl.ds(0, HALO)] = zeros

    @pl.when(t < tiles - 1)
    def _():
        to_left.wait_recv()

    @pl.when(t == tiles - 1)
    def _():
        ext[pl.ds(HALO + cells, HALO)] = zeros

    span = 128
    reach = span + 2 * HALO
    nbrs = neigh_ref.shape[0]
    for b in range(cells // span):
        lines = lax.broadcasted_iota(jnp.int32, (reach, span), 0) + b * span
        times = jnp.zeros((reach, span), F32)
        for k in range(nbrs):
            index = neigh_ref[pl.ds(k, 1), pl.ds(b * span, span)]
            times = times + jnp.where(lines == index, 1.0, 0.0)
        total = dot_tn(times.astype(BF16), ext[pl.ds(b * span, reach), :])
        gathered[pl.ds(b * span, span)] = (total / nbrs).astype(BF16)

    def teacher(rows):
        resid = state_ref[rows, :].astype(F32) + dot(gathered[rows, :], msg_ref[...])
        mean = jnp.mean(resid * resid, axis=1, keepdims=True)
        normed = (resid * lax.rsqrt(mean + 1e-06)).astype(BF16)
        up = dot(normed, up_ref[...])
        hidden = (up * jax.nn.sigmoid(up)).astype(BF16)
        out = (resid + dot(hidden, down_ref[...])).astype(BF16)
        teacher_ref[rows, :] = out
        return out

    for o in range(1, members):
        _, other = peer("member", o)
        teacher(pl.ds(pl.multiple_of(other * block, block), block))
        sent["teacher", o].start()
    t_all[pl.ds(0, block)] = teacher(own)

    for o in range(1, members):
        sent["state", o].wait_recv()
        sent["noise", o].wait_recv()
        student(o)
    for o in range(1, members):
        sent["teacher", o].wait_recv()

    chunk = 16
    scale = 1.0 / math.sqrt(cells * tiles)
    c_cross = 1.0 / (members * members)
    c_within = 1.0 / (members * (members - 1))

    def visit(i, losses):
        base = pl.multiple_of(i * chunk, chunk)
        rows = [pl.ds(pl.multiple_of(j * block + base, chunk), chunk) for j in range(members)]
        st = [s_all[r, :].astype(F32) for r in rows]
        te = [t_all[r, :].astype(F32) for r in rows]
        grads = [jnp.zeros((chunk, width), F32) for _ in rows]
        cross = jnp.zeros((chunk, width), F32)
        within = jnp.zeros((chunk, width), F32)
        for a in range(members):
            for b in range(members):
                d = st[a] - te[b]
                q = d * d + 0.01
                inv = lax.rsqrt(q)
                grads[a] = grads[a] + d * inv
                cross = cross + (q * inv - 0.1)
        grads = [g * c_cross for g in grads]
        for a in range(members):
            for b in range(a + 1, members):
                d = st[a] - st[b]
                q = d * d + 0.01
                inv = lax.rsqrt(q)
                slope = d * inv * c_within
                grads[a] = grads[a] - slope
                grads[b] = grads[b] + slope
                within = within + (q * inv - 0.1)
        for r, g in zip(rows, grads):
            g_all[r, :] = (g * scale).astype(BF16)
        return losses + (cross * c_cross - within * c_within)

    losses = lax.fori_loop(0, block // chunk, visit, jnp.zeros((chunk, width), F32))
    total = jnp.sum(losses, keepdims=True)
    lane = lax.broadcasted_iota(jnp.int32, (8, 128), 1)
    onehot = jnp.where(lane == region_ref[0], 1.0, 0.0) * total

    sig = jax.nn.sigmoid(pre_all[...])
    if not reduce_here:
        loss_ref[...] = onehot
        g = g_all[...]
        gout_ref[...] = dot_tn(sh_all[...], g)
        pre = pre_all[...]
        slope = sig * (1.0 + pre * (1.0 - sig))
        gpre = (dot_nt(g, sout_ref[...]) * slope).astype(BF16)
        gin_ref[...] = dot_tn(x_all[...], gpre)
        gnoise_ref[...] = dot_tn(n_all[...], gpre)
        for o in range(1, members):
            for what in ("state", "noise", "teacher"):
                sent[what, o].wait_send()
    else:
        bufs = list(bufs)
        loss_bufs = [bufs.pop(0) for _ in streams[0]]
        wire, part, land, share = [], [], [], []
        for order in streams:
            wire.append([bufs.pop(0) for _ in order])
            part.append([bufs.pop(0) for _ in order])
            land.append([bufs.pop(0) for _ in order])
            final = bufs.pop(0)
            share.append((final, bufs.pop(0)))
        column = width // members
        loss_now = [onehot]

        def start(s, k):
            step = streams[s][k]
            n = count_of(step, members)
            size = wire[s][k].shape[0] // n
            for o in range(1, n):
                device, other = peer(step, o)
                c = copy(
                    ("grad", s, k, o),
                    wire[s][k].at[pl.ds(other * size, size)],
                    land[s][k].at[o - 1],
                    device,
                )
                c.start()
                sent["grad", s, k, o] = c

        def finish(s, k):
            step = streams[s][k]
            n = count_of(step, members)
            size = wire[s][k].shape[0] // n
            mine = digit_of(step) * size
            for o in range(1, n):
                sent["grad", s, k, o].wait_recv()
            for i in range(size):
                value = part[s][k][mine + i]
                for o in range(1, n):
                    value = value + land[s][k][o - 1, i].astype(F32)
                if k + 1 < len(streams[s]):
                    part[s][k + 1][i] = value
                    wire[s][k + 1][i] = value.astype(BF16)
                else:
                    share[s][0][...] = value.astype(BF16)

        def start_loss(k):
            step = streams[0][k]
            mine = digit_of(step)
            loss_bufs[k][mine] = loss_now[0]
            for o in range(1, count_of(step, members)):
                device, _ = peer(step, o)
                c = copy(("loss", k, o), loss_bufs[k].at[mine], loss_bufs[k].at[mine], device)
                c.start()
                sent["loss", k, o] = c

        def finish_loss(k):
            n = count_of(streams[0][k], members)
            for o in range(1, n):
                sent["loss", k, o].wait_recv()
            value = loss_bufs[k][0]
            for j in range(1, n):
                value = value + loss_bufs[k][j]
            loss_now[0] = value

        def put(s, row, acc, member):
            rows = acc.shape[0] // tiles
            for j in range(tiles):
                slot = slot_of(streams[s], members, member, j)
                value = acc[j * rows : (j + 1) * rows]
                part[s][0][slot, row : row + rows] = value
                if rows % 16:
                    value = jnp.concatenate([value, jnp.zeros((-rows % 16, column), F32)])
                wire[s][0][slot, row : row + value.shape[0]] = value.astype(BF16)

        start_loss(0)
        for j in range(members):
            cols = pl.ds(j * column, column)
            put(0, 0, dot_tn(sh_all[...], g_all[:, cols]), j)
        start(0, 0)
        pre = pre_all[...]
        slope = sig * (1.0 + pre * (1.0 - sig))
        sh_all[...] = (dot_nt(g_all[...], sout_ref[...]) * slope).astype(BF16)
        rows_in = width // tiles
        for j in range(members):
            cols = pl.ds(j * column, column)
            put(1, 0, dot_tn(x_all[...], sh_all[:, cols]), j)
            put(1, rows_in, dot_tn(n_all[...], sh_all[:, cols]), j)
        start(1, 0)
        last = len(streams[0])
        for k in range(last):
            finish_loss(k)
            if k + 1 < last:
                start_loss(k + 1)
            for s in range(2):
                finish(s, k)
                if k + 1 < last:
                    start(s, k + 1)
                else:
                    for o in range(1, members):
                        device, _ = peer("member", o)
                        c = copy(("share", s, o), share[s][0], share[s][1].at[o - 1], device)
                        c.start()
                        sent["share", s, o] = c
        loss_ref[...] = loss_now[0] * (1.0 / (cells * tiles // REGIONS * width))

        def emit(s, value, member):
            cols = pl.ds(pl.multiple_of(member * column, column), column)
            if s == 0:
                gout_ref[:, cols] = value
            else:
                gin_ref[:, cols] = value[:rows_in]
                gnoise_ref[:, cols] = value[rows_in : rows_in + gnoise_ref.shape[0]]

        for s in range(2):
            emit(s, share[s][0][...].astype(F32), m)
            for o in range(1, members):
                sent["share", s, o].wait_recv()
                emit(s, share[s][1][o - 1].astype(F32), lax.rem(m + members - o, members))
        for c in sent.values():
            c.wait_send()

    @pl.when(t > 0)
    def _():
        to_left.wait_send()

    @pl.when(t < tiles - 1)
    def _():
        to_right.wait_send()


def on_device(members, tiles, *args):
    state, noise, neighbours, region_map = args[0][0], args[1][0], args[2], args[3]
    weights = args[4:]
    cells, width = state.shape
    draws = noise.shape[1]
    hidden = weights[3].shape[1]
    rows = [hidden // tiles, width // tiles, draws // tiles]
    column = width // members
    reduce_here = (
        rows[0] % 16 == 0
        and rows[1] % 16 == 0
        and rows[2] % 8 == 0
        and column % 128 == 0
        and hidden == width
        and tiles >= 8
        and members > 1
    )
    scratch = [
        pltpu.VMEM((cells + 2 * HALO, width), BF16),
        pltpu.VMEM((cells, width), BF16),
        pltpu.VMEM((cells, width), BF16),
        pltpu.VMEM((cells, draws), BF16),
        pltpu.VMEM((cells, width), BF16),
        pltpu.VMEM((cells, width), BF16),
        pltpu.VMEM((cells, hidden), F32),
        pltpu.VMEM((cells, hidden), BF16),
        pltpu.VMEM((cells, width), BF16),
        pltpu.SemaphoreType.DMA((len(layout(members, tiles)),)),
        pltpu.SemaphoreType.DMA((len(layout(members, tiles)),)),
    ]
    if reduce_here:
        shapes = ((rows[1], width), (rows[2], width), (rows[0], width))
        streams = orders(tiles)
        for step in streams[0]:
            scratch.append(pltpu.VMEM((count_of(step, members), 8, 128), F32))
        high = [rows[0], rows[1] + -(-rows[2] // 16) * 16]
        for order, tall in zip(streams, high):
            sizes = []
            left = members * tiles
            for step in order:
                sizes.append((left, count_of(step, members)))
                left //= count_of(step, members)
            scratch += [pltpu.VMEM((size, tall, column), BF16) for size, _ in sizes]
            scratch += [pltpu.VMEM((size, tall, column), F32) for size, _ in sizes]
            scratch += [pltpu.VMEM((n - 1, size // n, tall, column), BF16) for size, n in sizes]
            scratch.append(pltpu.VMEM((tall, column), BF16))
            scratch.append(pltpu.VMEM((members - 1, tall, column), BF16))
    else:
        shapes = ((width, hidden), (draws, hidden), (hidden, width))
    vmem = pl.BlockSpec(memory_space=pltpu.VMEM)
    teacher, loss, gin, gnoise, gout = pl.pallas_call(
        functools.partial(kernel, members, tiles, reduce_here),
        out_shape=[jax.ShapeDtypeStruct((cells, width), BF16), jax.ShapeDtypeStruct((8, 128), F32)]
        + [jax.ShapeDtypeStruct(s, F32) for s in shapes],
        in_specs=[vmem] * 3 + [pl.BlockSpec(memory_space=pltpu.SMEM)] + [vmem] * 6,
        out_specs=[vmem] * 5,
        scratch_shapes=scratch,
        compiler_params=pltpu.CompilerParams(
            collective_id=0, has_side_effects=True, vmem_limit_bytes=56 * 1024 * 1024
        ),
    )(state, noise, neighbours, region_map, *weights)
    region_loss = loss[0, :REGIONS]
    if not reduce_here:
        region_loss = lax.psum(region_loss, ("member", "tile")) / (cells * tiles // REGIONS * width)
        gin, gnoise, gout = lax.psum(
            tuple(
                lax.psum_scatter(g, "tile", scatter_dimension=0, tiled=True)
                for g in (gin, gnoise, gout)
            ),
            "member",
        )
    return teacher[None], region_loss, gin, gnoise, gout


def solution(mesh):
    in_specs = (
        P("member", "tile", None),
        P("member", "tile", None),
        P(None, "tile"),
        P("tile"),
        P(),
        P(),
        P(),
        P(),
        P(),
        P(),
    )
    out_specs = (P("member", "tile", None), P(), P("tile", None), P("tile", None), P("tile", None))
    return jax.shard_map(
        functools.partial(on_device, mesh.shape["member"], mesh.shape["tile"]),
        mesh=mesh,
        in_specs=in_specs,
        out_specs=out_specs,
        check_vma=False,
    )
```

```python
import functools
import math

import jax
import jax.numpy as jnp
from jax import lax
from jax.experimental import pallas as pl
from jax.experimental.pallas import tpu as pltpu
from jax.sharding import PartitionSpec as P

HALO = 64
REGIONS = 8
MESH = pl.DeviceIdType.MESH
F32 = jnp.float32
BF16 = jnp.bfloat16


def dot(a, b):
    return jnp.dot(a, b, preferred_element_type=F32)


def dot_tn(a, b):
    return lax.dot_general(a, b, (((0,), (0,)), ((), ())), preferred_element_type=F32)


def dot_nt(a, b):
    return lax.dot_general(a, b, (((1,), (1,)), ((), ())), preferred_element_type=F32)


def tile_digits(tiles):
    digits = []
    stride = 1
    for _ in range(2):
        if tiles // stride % 2 == 0 and tiles // stride > 2:
            digits.append((stride, 2))
            stride *= 2
    digits.append((stride, tiles // stride))
    return digits


def orders(tiles):
    digits = tile_digits(tiles)
    first = [digits[0], "member"] + digits[1:]
    second = digits[:2] + ["member"] + digits[2:]
    third = digits[:1] + digits[2:] + ["member"] + digits[1:2]
    return first, second, third


def count_of(step, members):
    return members if step == "member" else step[1]


def slot_of(order, members, member, tile):
    slot = 0
    for step in order:
        n = count_of(step, members)
        slot = slot * n + (member if step == "member" else tile // step[0] % n)
    return slot


def parts_of(block):
    return 2 if block % 32 == 0 else 1


def layout(members, tiles, parts):
    names = ["left", "right"]
    for o in range(1, members):
        names += [("state", o), ("noise", o)] + [("teacher", o, c) for c in range(parts)]
    for s, order in enumerate(orders(tiles)):
        for k, step in enumerate(order):
            for o in range(1, count_of(step, members)):
                names.append(("grad", s, k, o))
                if s == 0:
                    names.append(("loss", k, o))
        for o in range(1, members):
            names.append(("share", s, o))
    return {name: i for i, name in enumerate(names)}


def kernel(
    members,
    tiles,
    reduce_here,
    state_ref,
    noise_ref,
    neigh_ref,
    region_ref,
    msg_hbm,
    up_hbm,
    down_hbm,
    sin_hbm,
    snoise_hbm,
    sout_hbm,
    teacher_ref,
    loss_ref,
    gin_ref,
    gnoise_ref,
    gout_ref,
    ext,
    gathered,
    x_all,
    n_all,
    t_all,
    s_all,
    slope_all,
    sh_all,
    g_all,
    gpre_all,
    msg_ref,
    up_ref,
    down_ref,
    sin_ref,
    snoise_ref,
    sout_ref,
    load_sem,
    send_sem,
    recv_sem,
    *bufs,
):
    cells, width = state_ref.shape
    block = cells // members
    m = lax.axis_index("member")
    t = lax.axis_index("tile")
    parts = parts_of(block)
    part_rows = block // parts
    ids = layout(members, tiles, parts)
    streams = orders(tiles)

    def peer(step, o):
        if step == "member":
            other = lax.rem(m + o, members)
            return (other, t), other
        stride, n = step
        digit = lax.rem(t // stride, n)
        other = lax.rem(digit + o, n)
        return (m, t + (other - digit) * stride), other

    def digit_of(step):
        return m if step == "member" else lax.rem(t // step[0], step[1])

    def copy(name, src, dst, device):
        i = ids[name]
        return pltpu.make_async_remote_copy(
            src_ref=src,
            dst_ref=dst,
            send_sem=send_sem.at[i],
            recv_sem=recv_sem.at[i],
            device_id=device,
            device_id_type=MESH,
        )

    pairs = [
        (sin_hbm, sin_ref),
        (snoise_hbm, snoise_ref),
        (sout_hbm, sout_ref),
        (msg_hbm, msg_ref),
        (up_hbm, up_ref),
        (down_hbm, down_ref),
    ]
    loads = [pltpu.make_async_copy(a, b, load_sem.at[i]) for i, (a, b) in enumerate(pairs)]
    for load in loads:
        load.start()

    barrier = pltpu.get_barrier_semaphore()
    groups = ["member"] + (tile_digits(tiles) if reduce_here else [])
    waits = 0
    for step in groups:
        for o in range(1, count_of(step, members)):
            device, _ = peer(step, o)
            pl.semaphore_signal(barrier, inc=1, device_id=device, device_id_type=MESH)
            waits += 1

    @pl.when(t > 0)
    def _():
        pl.semaphore_signal(barrier, inc=1, device_id=(m, t - 1), device_id_type=MESH)

    @pl.when(t < tiles - 1)
    def _():
        pl.semaphore_signal(barrier, inc=1, device_id=(m, t + 1), device_id_type=MESH)

    ends = jnp.where(t > 0, 1, 0) + jnp.where(t < tiles - 1, 1, 0)
    pl.semaphore_wait(barrier, waits + ends)

    to_left = copy("left", state_ref.at[pl.ds(0, HALO)], ext.at[pl.ds(HALO + cells, HALO)], (m, t - 1))
    to_right = copy("right", state_ref.at[pl.ds(cells - HALO, HALO)], ext.at[pl.ds(0, HALO)], (m, t + 1))

    @pl.when(t > 0)
    def _():
        to_left.start()

    @pl.when(t < tiles - 1)
    def _():
        to_right.start()

    pending = []
    sent = {}
    for o in range(1, members):
        device, other = peer("member", o)
        rows = pl.ds(pl.multiple_of(other * block, block), block)
        slot = pl.ds(o * block, block)
        sent["state", o] = copy(("state", o), state_ref.at[rows], x_all.at[slot], device)
        sent["noise", o] = copy(("noise", o), noise_ref.at[rows], n_all.at[slot], device)
        sent["state", o].start()
        sent["noise", o].start()
        for c in range(parts):
            rows = pl.ds(pl.multiple_of(other * block + c * part_rows, part_rows), part_rows)
            slot = pl.ds(o * block + c * part_rows, part_rows)
            name = ("teacher", o, c)
            sent[name] = copy(name, teacher_ref.at[rows], t_all.at[slot], device)

    own = pl.ds(pl.multiple_of(m * block, block), block)
    x_all[pl.ds(0, block)] = state_ref[own, :]
    n_all[pl.ds(0, block)] = noise_ref[own, :]
    ext[pl.ds(HALO, cells)] = state_ref[...]

    def student(o):
        rows = pl.ds(o * block, block)
        x = x_all[rows, :]
        pre = dot(x, sin_ref[...]) + dot(n_all[rows, :], snoise_ref[...])
        sig = jax.nn.sigmoid(pre)
        slope_all[rows, :] = sig * (1.0 + pre * (1.0 - sig))
        sh = (pre * sig).astype(BF16)
        sh_all[rows, :] = sh
        s_all[rows, :] = (x.astype(F32) + dot(sh, sout_ref[...])).astype(BF16)

    for load in loads[:3]:
        load.wait()
    student(0)

    zeros = jnp.zeros((HALO, width), BF16)

    @pl.when(t > 0)
    def _():
        to_right.wait_recv()

    @pl.when(t == 0)
    def _():
        ext[pl.ds(0, HALO)] = zeros

    @pl.when(t < tiles - 1)
    def _():
        to_left.wait_recv()

    @pl.when(t == tiles - 1)
    def _():
        ext[pl.ds(HALO + cells, HALO)] = zeros

    span = 128
    reach = span + 2 * HALO
    nbrs = neigh_ref.shape[0]
    for b in range(cells // span):
        lines = lax.broadcasted_iota(jnp.int32, (reach, span), 0) + b * span
        times = jnp.zeros((reach, span), F32)
        for k in range(nbrs):
            index = neigh_ref[pl.ds(k, 1), pl.ds(b * span, span)]
            times = times + jnp.where(lines == index, 1.0, 0.0)
        total = dot_tn(times.astype(BF16), ext[pl.ds(b * span, reach), :])
        gathered[pl.ds(b * span, span)] = (total / nbrs).astype(BF16)

    def teacher(rows):
        resid = state_ref[rows, :].astype(F32) + dot(gathered[rows, :], msg_ref[...])
        mean = jnp.mean(resid * resid, axis=1, keepdims=True)
        normed = (resid * lax.rsqrt(mean + 1e-06)).astype(BF16)
        up = dot(normed, up_ref[...])
        hidden = (up * jax.nn.sigmoid(up)).astype(BF16)
        out = (resid + dot(hidden, down_ref[...])).astype(BF16)
        teacher_ref[rows, :] = out
        return out

    for load in loads[3:]:
        load.wait()
    for o in range(1, members):
        _, other = peer("member", o)
        teacher(pl.ds(pl.multiple_of(other * block, block), block))
        for c in range(parts):
            sent["teacher", o, c].start()
    t_all[pl.ds(0, block)] = teacher(own)

    for o in range(1, members):
        sent["state", o].wait_recv()
        sent["noise", o].wait_recv()
        student(o)
    chunk = 16
    scale = 1.0 / math.sqrt(cells * tiles)
    c_cross = 1.0 / (members * members)
    c_within = 1.0 / (members * (members - 1))

    def visit(i, losses):
        base = pl.multiple_of(i * chunk, chunk)
        rows = [pl.ds(pl.multiple_of(j * block + base, chunk), chunk) for j in range(members)]
        st = [s_all[r, :].astype(F32) for r in rows]
        te = [t_all[r, :].astype(F32) for r in rows]
        grads = [jnp.zeros((chunk, width), F32) for _ in rows]
        cross = jnp.zeros((chunk, width), F32)
        within = jnp.zeros((chunk, width), F32)
        for a in range(members):
            for b in range(members):
                d = st[a] - te[b]
                q = d * d + 0.01
                inv = lax.rsqrt(q)
                grads[a] = grads[a] + d * inv
                cross = cross + (q * inv - 0.1)
        grads = [g * c_cross for g in grads]
        for a in range(members):
            for b in range(a + 1, members):
                d = st[a] - st[b]
                q = d * d + 0.01
                inv = lax.rsqrt(q)
                slope = d * inv * c_within
                grads[a] = grads[a] - slope
                grads[b] = grads[b] + slope
                within = within + (q * inv - 0.1)
        for r, g in zip(rows, grads):
            g_all[r, :] = (g * scale).astype(BF16)
        return losses + (cross * c_cross - within * c_within)

    def backward(c):
        for j in range(members):
            rows = pl.ds(j * block + c * part_rows, part_rows)
            gpre_all[rows, :] = (dot_nt(g_all[rows, :], sout_ref[...]) * slope_all[rows, :]).astype(BF16)

    losses = jnp.zeros((chunk, width), F32)
    steps = part_rows // chunk
    for c in range(parts):
        for o in range(1, members):
            sent["teacher", o, c].wait_recv()
        losses = lax.fori_loop(c * steps, (c + 1) * steps, visit, losses)
        if c + 1 < parts:
            backward(c)
    total = jnp.sum(losses, keepdims=True)
    lane = lax.broadcasted_iota(jnp.int32, (8, 128), 1)
    onehot = jnp.where(lane == region_ref[0], 1.0, 0.0) * total

    if not reduce_here:
        loss_ref[...] = onehot
        gout_ref[...] = dot_tn(sh_all[...], g_all[...])
        backward(parts - 1)
        gin_ref[...] = dot_tn(x_all[...], gpre_all[...])
        gnoise_ref[...] = dot_tn(n_all[...], gpre_all[...])
        for c in sent.values():
            c.wait_send()
    else:
        bufs = list(bufs)
        loss_bufs = [bufs.pop(0) for _ in streams[0]]
        wire, part, land, share = [], [], [], []
        for order in streams:
            wire.append([bufs.pop(0) for _ in order])
            part.append([bufs.pop(0) for _ in order])
            land.append([bufs.pop(0) for _ in order])
            final = bufs.pop(0)
            share.append((final, bufs.pop(0)))
        column = width // members
        loss_now = [onehot]

        def start(s, k):
            step = streams[s][k]
            n = count_of(step, members)
            size = wire[s][k].shape[0] // n
            for o in range(1, n):
                device, other = peer(step, o)
                c = copy(
                    ("grad", s, k, o),
                    wire[s][k].at[pl.ds(other * size, size)],
                    land[s][k].at[o - 1],
                    device,
                )
                c.start()
                sent["grad", s, k, o] = c

        def finish(s, k):
            step = streams[s][k]
            n = count_of(step, members)
            size = wire[s][k].shape[0] // n
            mine = digit_of(step) * size
            for o in range(1, n):
                sent["grad", s, k, o].wait_recv()
            for i in range(size):
                value = part[s][k][mine + i]
                for o in range(1, n):
                    value = value + land[s][k][o - 1, i].astype(F32)
                if k + 1 < len(streams[s]):
                    part[s][k + 1][i] = value
                    wire[s][k + 1][i] = value.astype(BF16)
                else:
                    share[s][0][...] = value.astype(BF16)

        def start_loss(k):
            step = streams[0][k]
            mine = digit_of(step)
            loss_bufs[k][mine] = loss_now[0]
            for o in range(1, count_of(step, members)):
                device, _ = peer(step, o)
                c = copy(("loss", k, o), loss_bufs[k].at[mine], loss_bufs[k].at[mine], device)
                c.start()
                sent["loss", k, o] = c

        def finish_loss(k):
            n = count_of(streams[0][k], members)
            for o in range(1, n):
                sent["loss", k, o].wait_recv()
            value = loss_bufs[k][0]
            for j in range(1, n):
                value = value + loss_bufs[k][j]
            loss_now[0] = value

        def put(s, acc):
            rows = acc.shape[0] // tiles
            for i in range(members):
                for j in range(tiles):
                    slot = slot_of(streams[s], members, i, j)
                    value = acc[j * rows : (j + 1) * rows, i * column : (i + 1) * column]
                    if rows % 16:
                        value = jnp.concatenate([value, jnp.zeros((-rows % 16, column), F32)])
                    part[s][0][slot] = value
                    wire[s][0][slot] = value.astype(BF16)

        start_loss(0)
        put(0, dot_tn(sh_all[...], g_all[...]))
        start(0, 0)
        backward(parts - 1)
        put(1, dot_tn(x_all[...], gpre_all[...]))
        start(1, 0)
        put(2, dot_tn(n_all[...], gpre_all[...]))
        start(2, 0)
        last = len(streams[0])
        for k in range(last):
            finish_loss(k)
            if k + 1 < last:
                start_loss(k + 1)
            for s in range(len(streams)):
                finish(s, k)
                if k + 1 < last:
                    start(s, k + 1)
                else:
                    for o in range(1, members):
                        device, _ = peer("member", o)
                        c = copy(("share", s, o), share[s][0], share[s][1].at[o - 1], device)
                        c.start()
                        sent["share", s, o] = c
        loss_ref[...] = loss_now[0] * (1.0 / (cells * tiles // REGIONS * width))

        def emit(s, value, member):
            cols = pl.ds(pl.multiple_of(member * column, column), column)
            out = (gout_ref, gin_ref, gnoise_ref)[s]
            out[:, cols] = value[: out.shape[0]]

        for s in range(len(streams)):
            emit(s, share[s][0][...].astype(F32), m)
            for o in range(1, members):
                sent["share", s, o].wait_recv()
                emit(s, share[s][1][o - 1].astype(F32), lax.rem(m + members - o, members))
        for c in sent.values():
            c.wait_send()

    @pl.when(t > 0)
    def _():
        to_left.wait_send()

    @pl.when(t < tiles - 1)
    def _():
        to_right.wait_send()


def hand_on(*refs):
    loss_ref, region_ref, sem = refs[4], refs[9], refs[10]
    copies = [pltpu.make_async_copy(refs[i], refs[5 + i], sem.at[i]) for i in range(4)]
    for c in copies:
        c.start()
    region_ref[...] = loss_ref[0, : region_ref.shape[0]]
    for c in copies:
        c.wait()


def on_device(members, tiles, *args):
    state, noise, neighbours, region_map = args[0][0], args[1][0], args[2], args[3]
    weights = args[4:]
    cells, width = state.shape
    draws = noise.shape[1]
    hidden = weights[3].shape[1]
    rows = [hidden // tiles, width // tiles, draws // tiles]
    column = width // members
    reduce_here = (
        rows[0] % 16 == 0
        and rows[1] % 16 == 0
        and rows[2] % 8 == 0
        and column % 128 == 0
        and hidden == width
        and tiles >= 8
        and members > 1
    )
    scratch = [
        pltpu.VMEM((cells + 2 * HALO, width), BF16),
        pltpu.VMEM((cells, width), BF16),
        pltpu.VMEM((cells, width), BF16),
        pltpu.VMEM((cells, draws), BF16),
        pltpu.VMEM((cells, width), BF16),
        pltpu.VMEM((cells, width), BF16),
        pltpu.VMEM((cells, hidden), F32),
        pltpu.VMEM((cells, hidden), BF16),
        pltpu.VMEM((cells, width), BF16),
        pltpu.VMEM((cells, hidden), BF16),
    ]
    scratch += [pltpu.VMEM(w.shape, w.dtype) for w in weights]
    copies = len(layout(members, tiles, parts_of(cells // members)))
    scratch += [pltpu.SemaphoreType.DMA((n,)) for n in (len(weights), copies, copies)]
    if reduce_here:
        shapes = ((rows[1], width), (rows[2], width), (rows[0], width))
        streams = orders(tiles)
        for step in streams[0]:
            scratch.append(pltpu.VMEM((count_of(step, members), 8, 128), F32))
        high = [rows[0], rows[1], -(-rows[2] // 16) * 16]
        for order, tall in zip(streams, high):
            sizes = []
            left = members * tiles
            for step in order:
                sizes.append((left, count_of(step, members)))
                left //= count_of(step, members)
            scratch += [pltpu.VMEM((size, tall, column), BF16) for size, _ in sizes]
            scratch += [pltpu.VMEM((size, tall, column), F32) for size, _ in sizes]
            scratch += [pltpu.VMEM((n - 1, size // n, tall, column), BF16) for size, n in sizes]
            scratch.append(pltpu.VMEM((tall, column), BF16))
            scratch.append(pltpu.VMEM((members - 1, tall, column), BF16))
    else:
        shapes = ((width, hidden), (draws, hidden), (hidden, width))
    vmem = pl.BlockSpec(memory_space=pltpu.VMEM)
    teacher, loss, gin, gnoise, gout = pl.pallas_call(
        functools.partial(kernel, members, tiles, reduce_here),
        out_shape=[jax.ShapeDtypeStruct((cells, width), BF16), jax.ShapeDtypeStruct((8, 128), F32)]
        + [jax.ShapeDtypeStruct(s, F32) for s in shapes],
        in_specs=[vmem] * 3 + [pl.BlockSpec(memory_space=pltpu.SMEM)]
        + [pl.BlockSpec(memory_space=pl.ANY)] * 6,
        out_specs=[vmem] * 5,
        scratch_shapes=scratch,
        compiler_params=pltpu.CompilerParams(
            collective_id=0, has_side_effects=True, vmem_limit_bytes=56 * 1024 * 1024
        ),
    )(state, noise, neighbours, region_map, *weights)
    if reduce_here:
        hbm = pl.BlockSpec(memory_space=pl.ANY)
        big = (teacher, gin, gnoise, gout)
        teacher, gin, gnoise, gout, region_loss = pl.pallas_call(
            hand_on,
            out_shape=[jax.ShapeDtypeStruct(a.shape, a.dtype) for a in big]
            + [jax.ShapeDtypeStruct((REGIONS,), F32)],
            in_specs=[hbm] * 4 + [vmem],
            out_specs=[hbm] * 4 + [vmem],
            scratch_shapes=[pltpu.SemaphoreType.DMA((4,))],
        )(*big, loss)
    else:
        region_loss = loss[0, :REGIONS]
        region_loss = lax.psum(region_loss, ("member", "tile")) / (cells * tiles // REGIONS * width)
        gin, gnoise, gout = lax.psum(
            tuple(
                lax.psum_scatter(g, "tile", scatter_dimension=0, tiled=True)
                for g in (gin, gnoise, gout)
            ),
            "member",
        )
    return teacher[None], region_loss, gin, gnoise, gout


def solution(mesh):
    in_specs = (
        P("member", "tile", None),
        P("member", "tile", None),
        P(None, "tile"),
        P("tile"),
        P(),
        P(),
        P(),
        P(),
        P(),
        P(),
    )
    out_specs = (P("member", "tile", None), P(), P("tile", None), P("tile", None), P("tile", None))
    return jax.shard_map(
        functools.partial(on_device, mesh.shape["member"], mesh.shape["tile"]),
        mesh=mesh,
        in_specs=in_specs,
        out_specs=out_specs,
        check_vma=False,
    )
```

```python
import functools
import math

import jax
import jax.numpy as jnp
from jax import lax
from jax.experimental import pallas as pl
from jax.experimental.pallas import tpu as pltpu
from jax.sharding import PartitionSpec as P

HALO = 64
REGIONS = 8
MESH = pl.DeviceIdType.MESH
F32 = jnp.float32
BF16 = jnp.bfloat16


def dot(a, b):
    return jnp.dot(a, b, preferred_element_type=F32)


def dot_tn(a, b):
    return lax.dot_general(a, b, (((0,), (0,)), ((), ())), preferred_element_type=F32)


def dot_nt(a, b):
    return lax.dot_general(a, b, (((1,), (1,)), ((), ())), preferred_element_type=F32)


def tile_digits(tiles):
    digits = []
    stride = 1
    for _ in range(2):
        if tiles // stride % 2 == 0 and tiles // stride > 2:
            digits.append((stride, 2))
            stride *= 2
    digits.append((stride, tiles // stride))
    return digits


def orders(tiles):
    digits = tile_digits(tiles)
    first = [digits[0], "member"] + digits[1:]
    second = digits
    third = digits[:1] + digits[2:] + digits[1:2]
    return first, second, third


def count_of(step, members):
    return members if step == "member" else step[1]


def slot_of(order, members, member, tile):
    slot = 0
    for step in order:
        n = count_of(step, members)
        slot = slot * n + (member if step == "member" else tile // step[0] % n)
    return slot


def parts_of(block):
    return 2 if block % 32 == 0 else 1


def layout(members, tiles, parts):
    names = ["left", "right"]
    for o in range(1, members):
        names += [("state", o), ("noise", o)] + [("teacher", o, c) for c in range(parts)]
    for s, order in enumerate(orders(tiles)):
        for k, step in enumerate(order):
            for o in range(1, count_of(step, members)):
                names.append(("grad", s, k, o))
                if s == 0:
                    names.append(("loss", k, o))
        for o in range(1, members):
            names.append(("share", s, o))
    return {name: i for i, name in enumerate(names)}


def kernel(
    members,
    tiles,
    reduce_here,
    state_ref,
    noise_ref,
    neigh_ref,
    region_ref,
    msg_hbm,
    up_hbm,
    down_hbm,
    sin_hbm,
    snoise_hbm,
    sout_hbm,
    teacher_ref,
    loss_ref,
    gin_ref,
    gnoise_ref,
    gout_ref,
    ext,
    gathered,
    x_all,
    n_all,
    t_all,
    s_all,
    slope_all,
    sh_all,
    g_all,
    gpre_all,
    msg_ref,
    up_ref,
    down_ref,
    sin_ref,
    snoise_ref,
    sout_ref,
    load_sem,
    send_sem,
    recv_sem,
    *bufs,
):
    cells, width = state_ref.shape
    block = cells // members
    m = lax.axis_index("member")
    t = lax.axis_index("tile")
    parts = parts_of(block)
    part_rows = block // parts
    ids = layout(members, tiles, parts)
    streams = orders(tiles)

    def peer(step, o):
        if step == "member":
            other = lax.rem(m + o, members)
            return (other, t), other
        stride, n = step
        digit = lax.rem(t // stride, n)
        other = lax.rem(digit + o, n)
        return (m, t + (other - digit) * stride), other

    def digit_of(step):
        return m if step == "member" else lax.rem(t // step[0], step[1])

    def copy(name, src, dst, device):
        i = ids[name]
        return pltpu.make_async_remote_copy(
            src_ref=src,
            dst_ref=dst,
            send_sem=send_sem.at[i],
            recv_sem=recv_sem.at[i],
            device_id=device,
            device_id_type=MESH,
        )

    pairs = [
        (sin_hbm, sin_ref),
        (snoise_hbm, snoise_ref),
        (sout_hbm, sout_ref),
        (msg_hbm, msg_ref),
        (up_hbm, up_ref),
        (down_hbm, down_ref),
    ]
    loads = [pltpu.make_async_copy(a, b, load_sem.at[i]) for i, (a, b) in enumerate(pairs)]
    for load in loads:
        load.start()

    barrier = pltpu.get_barrier_semaphore()
    groups = ["member"] + (tile_digits(tiles) if reduce_here else [])
    waits = 0
    for step in groups:
        for o in range(1, count_of(step, members)):
            device, _ = peer(step, o)
            pl.semaphore_signal(barrier, inc=1, device_id=device, device_id_type=MESH)
            waits += 1

    @pl.when(t > 0)
    def _():
        pl.semaphore_signal(barrier, inc=1, device_id=(m, t - 1), device_id_type=MESH)

    @pl.when(t < tiles - 1)
    def _():
        pl.semaphore_signal(barrier, inc=1, device_id=(m, t + 1), device_id_type=MESH)

    ends = jnp.where(t > 0, 1, 0) + jnp.where(t < tiles - 1, 1, 0)
    pl.semaphore_wait(barrier, waits + ends)

    to_left = copy("left", state_ref.at[pl.ds(0, HALO)], ext.at[pl.ds(HALO + cells, HALO)], (m, t - 1))
    to_right = copy("right", state_ref.at[pl.ds(cells - HALO, HALO)], ext.at[pl.ds(0, HALO)], (m, t + 1))

    @pl.when(t > 0)
    def _():
        to_left.start()

    @pl.when(t < tiles - 1)
    def _():
        to_right.start()

    pending = []
    sent = {}
    for o in range(1, members):
        device, other = peer("member", o)
        rows = pl.ds(pl.multiple_of(other * block, block), block)
        slot = pl.ds(o * block, block)
        sent["state", o] = copy(("state", o), state_ref.at[rows], x_all.at[slot], device)
        sent["noise", o] = copy(("noise", o), noise_ref.at[rows], n_all.at[slot], device)
        sent["state", o].start()
        sent["noise", o].start()
        for c in range(parts):
            rows = pl.ds(pl.multiple_of(other * block + c * part_rows, part_rows), part_rows)
            slot = pl.ds(o * block + c * part_rows, part_rows)
            name = ("teacher", o, c)
            sent[name] = copy(name, teacher_ref.at[rows], t_all.at[slot], device)

    own = pl.ds(pl.multiple_of(m * block, block), block)
    x_all[pl.ds(0, block)] = state_ref[own, :]
    n_all[pl.ds(0, block)] = noise_ref[own, :]
    ext[pl.ds(HALO, cells)] = state_ref[...]

    def student(o):
        rows = pl.ds(o * block, block)
        x = x_all[rows, :]
        pre = dot(x, sin_ref[...]) + dot(n_all[rows, :], snoise_ref[...])
        sig = jax.nn.sigmoid(pre)
        slope_all[rows, :] = sig * (1.0 + pre * (1.0 - sig))
        sh = (pre * sig).astype(BF16)
        sh_all[rows, :] = sh
        s_all[rows, :] = (x.astype(F32) + dot(sh, sout_ref[...])).astype(BF16)

    for load in loads[:3]:
        load.wait()
    student(0)

    zeros = jnp.zeros((HALO, width), BF16)

    @pl.when(t > 0)
    def _():
        to_right.wait_recv()

    @pl.when(t == 0)
    def _():
        ext[pl.ds(0, HALO)] = zeros

    @pl.when(t < tiles - 1)
    def _():
        to_left.wait_recv()

    @pl.when(t == tiles - 1)
    def _():
        ext[pl.ds(HALO + cells, HALO)] = zeros

    span = 128
    reach = span + 2 * HALO
    nbrs = neigh_ref.shape[0]
    for b in range(cells // span):
        lines = lax.broadcasted_iota(jnp.int32, (reach, span), 0) + b * span
        times = jnp.zeros((reach, span), F32)
        for k in range(nbrs):
            index = neigh_ref[pl.ds(k, 1), pl.ds(b * span, span)]
            times = times + jnp.where(lines == index, 1.0, 0.0)
        total = dot_tn(times.astype(BF16), ext[pl.ds(b * span, reach), :])
        gathered[pl.ds(b * span, span)] = (total / nbrs).astype(BF16)

    def teacher(rows):
        resid = state_ref[rows, :].astype(F32) + dot(gathered[rows, :], msg_ref[...])
        mean = jnp.mean(resid * resid, axis=1, keepdims=True)
        normed = (resid * lax.rsqrt(mean + 1e-06)).astype(BF16)
        up = dot(normed, up_ref[...])
        hidden = (up * jax.nn.sigmoid(up)).astype(BF16)
        out = (resid + dot(hidden, down_ref[...])).astype(BF16)
        teacher_ref[rows, :] = out
        return out

    for load in loads[3:]:
        load.wait()
    for o in range(1, members):
        _, other = peer("member", o)
        teacher(pl.ds(pl.multiple_of(other * block, block), block))
        for c in range(parts):
            sent["teacher", o, c].start()
    t_all[pl.ds(0, block)] = teacher(own)

    for o in range(1, members):
        sent["state", o].wait_recv()
        sent["noise", o].wait_recv()
        student(o)
    chunk = 16
    lanes = 256 if width % 256 == 0 else width
    scale = 1.0 / math.sqrt(cells * tiles)
    c_cross = 1.0 / (members * members)
    c_within = 1.0 / (members * (members - 1))

    def visit(i, losses):
        base = pl.multiple_of(i * chunk, chunk)
        rows = [pl.ds(pl.multiple_of(j * block + base, chunk), chunk) for j in range(members)]
        for at in range(0, width, lanes):
            cols = pl.ds(at, lanes)
            st = [s_all[r, cols].astype(F32) for r in rows]
            te = [t_all[r, cols].astype(F32) for r in rows]
            grads = [jnp.zeros((chunk, lanes), F32) for _ in rows]
            cross = jnp.zeros((chunk, lanes), F32)
            within = jnp.zeros((chunk, lanes), F32)
            for a in range(members):
                for b in range(members):
                    d = st[a] - te[b]
                    q = d * d + 0.01
                    inv = lax.rsqrt(q)
                    grads[a] = grads[a] + d * inv
                    cross = cross + (q * inv - 0.1)
            grads = [g * c_cross for g in grads]
            for a in range(members):
                for b in range(a + 1, members):
                    d = st[a] - st[b]
                    q = d * d + 0.01
                    inv = lax.rsqrt(q)
                    slope = d * inv * c_within
                    grads[a] = grads[a] - slope
                    grads[b] = grads[b] + slope
                    within = within + (q * inv - 0.1)
            for r, g in zip(rows, grads):
                g_all[r, cols] = (g * scale).astype(BF16)
            losses = losses + (cross * c_cross - within * c_within)
        return losses

    def backward(c):
        for j in range(members):
            rows = pl.ds(j * block + c * part_rows, part_rows)
            gpre_all[rows, :] = (dot_nt(g_all[rows, :], sout_ref[...]) * slope_all[rows, :]).astype(BF16)

    losses = jnp.zeros((chunk, lanes), F32)
    steps = part_rows // chunk
    for c in range(parts):
        for o in range(1, members):
            sent["teacher", o, c].wait_recv()
        losses = lax.fori_loop(c * steps, (c + 1) * steps, visit, losses)
        if c + 1 < parts:
            backward(c)
    total = jnp.sum(losses, keepdims=True)
    lane = lax.broadcasted_iota(jnp.int32, (8, 128), 1)
    onehot = jnp.where(lane == region_ref[...], 1.0, 0.0) * total

    if not reduce_here:
        loss_ref[...] = onehot
        gout_ref[...] = dot_tn(sh_all[...], g_all[...])
        backward(parts - 1)
        gin_ref[...] = dot_tn(x_all[...], gpre_all[...])
        gnoise_ref[...] = dot_tn(n_all[...], gpre_all[...])
        for c in sent.values():
            c.wait_send()
    else:
        bufs = list(bufs)
        loss_bufs = [bufs.pop(0) for _ in streams[0]]
        wire, part, land, share = [], [], [], []
        for order in streams:
            wire.append([bufs.pop(0) for _ in order])
            part.append([bufs.pop(0) for _ in order])
            land.append([bufs.pop(0) for _ in order])
            share.append(bufs.pop(0))
        column = width // members
        loss_now = [onehot]

        def start(s, k):
            step = streams[s][k]
            n = count_of(step, members)
            size = wire[s][k].shape[0] // n
            for o in range(1, n):
                device, other = peer(step, o)
                c = copy(
                    ("grad", s, k, o),
                    wire[s][k].at[pl.ds(other * size, size)],
                    land[s][k].at[o - 1],
                    device,
                )
                c.start()
                sent["grad", s, k, o] = c

        def finish(s, k):
            step = streams[s][k]
            n = count_of(step, members)
            size = wire[s][k].shape[0] // n
            mine = digit_of(step) * size
            for o in range(1, n):
                sent["grad", s, k, o].wait_recv()
            for i in range(size):
                value = part[s][k][mine + i]
                for o in range(1, n):
                    value = value + land[s][k][o - 1, i].astype(F32)
                if k + 1 < len(streams[s]):
                    part[s][k + 1][i] = value
                    wire[s][k + 1][i] = value.astype(BF16)
                else:
                    share[s][m] = value.astype(BF16)

        def start_loss(k):
            step = streams[0][k]
            mine = digit_of(step)
            loss_bufs[k][mine] = loss_now[0]
            for o in range(1, count_of(step, members)):
                device, _ = peer(step, o)
                c = copy(("loss", k, o), loss_bufs[k].at[mine], loss_bufs[k].at[mine], device)
                c.start()
                sent["loss", k, o] = c

        def finish_loss(k):
            n = count_of(streams[0][k], members)
            for o in range(1, n):
                sent["loss", k, o].wait_recv()
            value = loss_bufs[k][0]
            for j in range(1, n):
                value = value + loss_bufs[k][j]
            loss_now[0] = value

        def put(s, acc):
            rows = acc.shape[0] // tiles
            span = column if "member" in streams[s] else width
            for i in range(width // span):
                for j in range(tiles):
                    slot = slot_of(streams[s], members, i, j)
                    value = acc[j * rows : (j + 1) * rows, i * span : (i + 1) * span]
                    if rows % 16:
                        value = jnp.concatenate([value[:, : span // 2], value[:, span // 2 :]])
                    part[s][0][slot] = value
                    wire[s][0][slot] = value.astype(BF16)

        start_loss(0)
        put(0, dot_tn(sh_all[...], g_all[...]))
        start(0, 0)
        backward(parts - 1)
        put(1, dot_tn(x_all[...], gpre_all[...]))
        start(1, 0)
        finish(0, 0)
        start(0, 1)
        put(2, dot_tn(n_all[...], gpre_all[...]))
        start(2, 0)

        def start_share(s):
            for o in range(1, members):
                device, _ = peer("member", o)
                c = copy(("share", s, o), share[s].at[m], share[s].at[m], device)
                c.start()
                sent["share", s, o] = c

        for k in range(len(streams[0])):
            finish_loss(k)
            if k + 1 < len(streams[0]):
                start_loss(k + 1)
            for s in range(len(streams)):
                if k < len(streams[s]):
                    if (s, k) != (0, 0):
                        finish(s, k)
                        if k + 1 < len(streams[s]):
                            start(s, k + 1)
                        else:
                            start_share(s)
        loss_ref[...] = loss_now[0] * (1.0 / (cells * tiles // REGIONS * width))
        for s in (1, 2, 0):
            for o in range(1, members):
                sent["share", s, o].wait_recv()
            pieces = [share[s][j].astype(F32) for j in range(members)]
            if s == 0:
                for j in range(members):
                    gout_ref[:, j * column : (j + 1) * column] = pieces[j]
            else:
                total = sum(pieces[1:], pieces[0])
                if s == 1:
                    gin_ref[...] = total
                else:
                    rows = gnoise_ref.shape[0]
                    if rows % 16:
                        total = jnp.concatenate([total[:rows], total[rows:]], axis=1)
                    gnoise_ref[...] = total
        for c in sent.values():
            c.wait_send()

    @pl.when(t > 0)
    def _():
        to_left.wait_send()

    @pl.when(t < tiles - 1)
    def _():
        to_right.wait_send()


def hand_on(*refs):
    for i in range(4):
        refs[5 + i][...] = refs[i][...]
    refs[9][...] = refs[4][0, : refs[9].shape[0]]


def on_device(members, tiles, *args):
    state, noise, neighbours, region_map = args[0][0], args[1][0], args[2], args[3]
    weights = args[4:]
    cells, width = state.shape
    draws = noise.shape[1]
    hidden = weights[3].shape[1]
    rows = [hidden // tiles, width // tiles, draws // tiles]
    column = width // members
    reduce_here = (
        rows[0] % 16 == 0
        and rows[1] % 16 == 0
        and rows[2] % 8 == 0
        and column % 128 == 0
        and hidden == width
        and tiles >= 8
        and members > 1
    )
    scratch = [
        pltpu.VMEM((cells + 2 * HALO, width), BF16),
        pltpu.VMEM((cells, width), BF16),
        pltpu.VMEM((cells, width), BF16),
        pltpu.VMEM((cells, draws), BF16),
        pltpu.VMEM((cells, width), BF16),
        pltpu.VMEM((cells, width), BF16),
        pltpu.VMEM((cells, hidden), F32),
        pltpu.VMEM((cells, hidden), BF16),
        pltpu.VMEM((cells, width), BF16),
        pltpu.VMEM((cells, hidden), BF16),
    ]
    scratch += [pltpu.VMEM(w.shape, w.dtype) for w in weights]
    copies = len(layout(members, tiles, parts_of(cells // members)))
    scratch += [pltpu.SemaphoreType.DMA((n,)) for n in (len(weights), copies, copies)]
    if reduce_here:
        shapes = ((rows[1], width), (rows[2], width), (rows[0], width))
        streams = orders(tiles)
        for step in streams[0]:
            scratch.append(pltpu.VMEM((count_of(step, members), 8, 128), F32))
        noise_piece = (2 * rows[2], width // 2) if rows[2] % 16 else (rows[2], width)
        pieces = [(rows[0], column), (rows[1], width), noise_piece]
        for order, piece in zip(streams, pieces):
            sizes = []
            left = (members if "member" in order else 1) * tiles
            for step in order:
                sizes.append((left, count_of(step, members)))
                left //= count_of(step, members)
            scratch += [pltpu.VMEM((size,) + piece, BF16) for size, _ in sizes]
            scratch += [pltpu.VMEM((size,) + piece, F32) for size, _ in sizes]
            scratch += [pltpu.VMEM((n - 1, size // n) + piece, BF16) for size, n in sizes]
            scratch.append(pltpu.VMEM((members,) + piece, BF16))
    else:
        shapes = ((width, hidden), (draws, hidden), (hidden, width))
    vmem = pl.BlockSpec(memory_space=pltpu.VMEM)
    teacher, loss, gin, gnoise, gout = pl.pallas_call(
        functools.partial(kernel, members, tiles, reduce_here),
        out_shape=[jax.ShapeDtypeStruct((cells, width), BF16), jax.ShapeDtypeStruct((8, 128), F32)]
        + [jax.ShapeDtypeStruct(s, F32) for s in shapes],
        in_specs=[vmem] * 3 + [vmem]
        + [pl.BlockSpec(memory_space=pl.ANY)] * 6,
        out_specs=[vmem] * 5,
        scratch_shapes=scratch,
        compiler_params=pltpu.CompilerParams(
            collective_id=0, has_side_effects=True, vmem_limit_bytes=56 * 1024 * 1024
        ),
    )(state, noise, neighbours, region_map.reshape(1, 1), *weights)
    if reduce_here:
        big = (teacher, gin, gnoise, gout)
        teacher, gin, gnoise, gout, region_loss = pl.pallas_call(
            hand_on,
            out_shape=[jax.ShapeDtypeStruct(a.shape, a.dtype) for a in big]
            + [jax.ShapeDtypeStruct((REGIONS,), F32)],
            in_specs=[vmem] * 5,
            out_specs=[vmem] * 5,
        )(*big, loss)
    else:
        region_loss = loss[0, :REGIONS]
        region_loss = lax.psum(region_loss, ("member", "tile")) / (cells * tiles // REGIONS * width)
        gin, gnoise, gout = lax.psum(
            tuple(
                lax.psum_scatter(g, "tile", scatter_dimension=0, tiled=True)
                for g in (gin, gnoise, gout)
            ),
            "member",
        )
    return teacher[None], region_loss, gin, gnoise, gout


def solution(mesh):
    in_specs = (
        P("member", "tile", None),
        P("member", "tile", None),
        P(None, "tile"),
        P("tile"),
        P(),
        P(),
        P(),
        P(),
        P(),
        P(),
    )
    out_specs = (P("member", "tile", None), P(), P("tile", None), P("tile", None), P("tile", None))
    return jax.shard_map(
        functools.partial(on_device, mesh.shape["member"], mesh.shape["tile"]),
        mesh=mesh,
        in_specs=in_specs,
        out_specs=out_specs,
        check_vma=False,
    )
```

```python
import functools
import math

import jax
import jax.numpy as jnp
from jax import lax
from jax.experimental import pallas as pl
from jax.experimental.pallas import tpu as pltpu
from jax.sharding import PartitionSpec as P

HALO = 64
REGIONS = 8
MESH = pl.DeviceIdType.MESH
F32 = jnp.float32
BF16 = jnp.bfloat16


def dot(a, b):
    return jnp.dot(a, b, preferred_element_type=F32)


def dot_tn(a, b):
    return lax.dot_general(a, b, (((0,), (0,)), ((), ())), preferred_element_type=F32)


def tile_digits(tiles):
    digits = []
    stride = 1
    for _ in range(2):
        if tiles // stride % 2 == 0 and tiles // stride > 2:
            digits.append((stride, 2))
            stride *= 2
    digits.append((stride, tiles // stride))
    return digits


def orders(tiles):
    digits = tile_digits(tiles)
    first = [digits[0], "member"] + digits[1:]
    second = digits
    third = digits[:1] + digits[2:] + digits[1:2]
    return first, second, third


def count_of(step, members):
    return members if step == "member" else step[1]


def slot_of(order, members, member, tile):
    slot = 0
    for step in order:
        n = count_of(step, members)
        slot = slot * n + (member if step == "member" else tile // step[0] % n)
    return slot


def parts_of(block):
    return 4 if block % 64 == 0 else 1


def layout(members, tiles, parts):
    names = ["left", "right"]
    for o in range(1, members):
        names += [("state", o), ("noise", o)] + [("teacher", o, c) for c in range(parts)]
    for s, order in enumerate(orders(tiles)):
        for k, step in enumerate(order):
            for o in range(1, count_of(step, members)):
                names.append(("grad", s, k, o))
                if s == 0:
                    names.append(("loss", k, o))
        for o in range(1, members):
            names.append(("share", s, o))
    return {name: i for i, name in enumerate(names)}


def kernel(
    members,
    tiles,
    reduce_here,
    state_hbm,
    noise_hbm,
    neigh_hbm,
    region_hbm,
    msg_hbm,
    up_hbm,
    down_hbm,
    sin_hbm,
    snoise_hbm,
    sout_hbm,
    teacher_hbm,
    loss_ref,
    gin_ref,
    gnoise_ref,
    gout_ref,
    ext,
    gathered,
    x_all,
    n_all,
    t_all,
    s_all,
    slope_all,
    sh_all,
    g_all,
    gpre_all,
    x_turned,
    n_turned,
    sh_turned,
    sout_turned,
    teacher_ref,
    neigh_ref,
    region_ref,
    msg_ref,
    up_ref,
    down_ref,
    sin_ref,
    snoise_ref,
    sout_ref,
    load_sem,
    send_sem,
    recv_sem,
    *bufs,
):
    cells, width = state_hbm.shape
    block = cells // members
    m = lax.axis_index("member")
    t = lax.axis_index("tile")
    parts = parts_of(block)
    part_rows = block // parts
    ids = layout(members, tiles, parts)
    streams = orders(tiles)

    def peer(step, o):
        if step == "member":
            other = lax.rem(m + o, members)
            return (other, t), other
        stride, n = step
        digit = lax.rem(t // stride, n)
        other = lax.rem(digit + o, n)
        return (m, t + (other - digit) * stride), other

    def digit_of(step):
        return m if step == "member" else lax.rem(t // step[0], step[1])

    def copy(name, src, dst, device):
        i = ids[name]
        return pltpu.make_async_remote_copy(
            src_ref=src,
            dst_ref=dst,
            send_sem=send_sem.at[i],
            recv_sem=recv_sem.at[i],
            device_id=device,
            device_id_type=MESH,
        )

    own = pl.ds(pl.multiple_of(m * block, block), block)
    pairs = [
        (state_hbm.at[own], x_all.at[pl.ds(0, block)]),
        (noise_hbm.at[own], n_all.at[pl.ds(0, block)]),
        (sin_hbm, sin_ref),
        (snoise_hbm, snoise_ref),
        (sout_hbm, sout_ref),
        (state_hbm, ext.at[pl.ds(HALO, cells)]),
        (neigh_hbm, neigh_ref),
        (msg_hbm, msg_ref),
        (up_hbm, up_ref),
        (down_hbm, down_ref),
        (region_hbm, region_ref),
    ]
    barrier = pltpu.get_barrier_semaphore()
    groups = ["member"] + (tile_digits(tiles) if reduce_here else [])
    waits = 0
    for step in groups:
        for o in range(1, count_of(step, members)):
            device, _ = peer(step, o)
            pl.semaphore_signal(barrier, inc=1, device_id=device, device_id_type=MESH)
            waits += 1

    @pl.when(t > 0)
    def _():
        pl.semaphore_signal(barrier, inc=1, device_id=(m, t - 1), device_id_type=MESH)

    @pl.when(t < tiles - 1)
    def _():
        pl.semaphore_signal(barrier, inc=1, device_id=(m, t + 1), device_id_type=MESH)

    loads = [pltpu.make_async_copy(a, b, load_sem.at[i]) for i, (a, b) in enumerate(pairs)]
    for load in loads:
        load.start()
    ends = jnp.where(t > 0, 1, 0) + jnp.where(t < tiles - 1, 1, 0)
    pl.semaphore_wait(barrier, waits + ends)

    to_left = copy("left", state_hbm.at[pl.ds(0, HALO)], ext.at[pl.ds(HALO + cells, HALO)], (m, t - 1))
    to_right = copy("right", state_hbm.at[pl.ds(cells - HALO, HALO)], ext.at[pl.ds(0, HALO)], (m, t + 1))

    @pl.when(t > 0)
    def _():
        to_left.start()

    @pl.when(t < tiles - 1)
    def _():
        to_right.start()

    pending = []
    sent = {}
    for o in range(1, members):
        device, other = peer("member", o)
        rows = pl.ds(pl.multiple_of(other * block, block), block)
        slot = pl.ds(o * block, block)
        sent["state", o] = copy(("state", o), state_hbm.at[rows], x_all.at[slot], device)
        sent["noise", o] = copy(("noise", o), noise_hbm.at[rows], n_all.at[slot], device)
        sent["state", o].start()
        sent["noise", o].start()
        for c in range(parts):
            rows = pl.ds(pl.multiple_of(other * block + c * part_rows, part_rows), part_rows)
            slot = pl.ds(o * block + c * part_rows, part_rows)
            name = ("teacher", o, c)
            sent[name] = copy(name, teacher_ref.at[rows], t_all.at[slot], device)

    def student(o):
        rows = pl.ds(o * block, block)
        x = x_all[rows, :]
        pre = dot(x, sin_ref[...]) + dot(n_all[rows, :], snoise_ref[...])
        sig = jax.nn.sigmoid(pre)
        slope_all[rows, :] = sig * (1.0 + pre * (1.0 - sig))
        sh = (pre * sig).astype(BF16)
        sh_all[rows, :] = sh
        s_all[rows, :] = (x.astype(F32) + dot(sh, sout_ref[...])).astype(BF16)

    for load in loads[:5]:
        load.wait()
    student(0)

    zeros = jnp.zeros((HALO, width), BF16)

    @pl.when(t > 0)
    def _():
        to_right.wait_recv()

    @pl.when(t == 0)
    def _():
        ext[pl.ds(0, HALO)] = zeros

    @pl.when(t < tiles - 1)
    def _():
        to_left.wait_recv()

    @pl.when(t == tiles - 1)
    def _():
        ext[pl.ds(HALO + cells, HALO)] = zeros

    for load in loads[5:]:
        load.wait()

    span = 128
    reach = span + 2 * HALO
    nbrs = neigh_ref.shape[0]
    for b in range(cells // span):
        lines = lax.broadcasted_iota(jnp.int32, (reach, span), 0) + b * span
        times = jnp.zeros((reach, span), F32)
        for k in range(nbrs):
            index = neigh_ref[pl.ds(k, 1), pl.ds(b * span, span)]
            times = times + jnp.where(lines == index, 1.0, 0.0)
        total = dot_tn(times.astype(BF16), ext[pl.ds(b * span, reach), :])
        gathered[pl.ds(b * span, span)] = (total / nbrs).astype(BF16)

    def teacher(at):
        rows = pl.ds(at, block)
        resid = ext[pl.ds(at + HALO, block), :].astype(F32) + dot(gathered[rows, :], msg_ref[...])
        mean = jnp.mean(resid * resid, axis=1, keepdims=True)
        normed = (resid * lax.rsqrt(mean + 1e-06)).astype(BF16)
        up = dot(normed, up_ref[...])
        hidden = (up * jax.nn.sigmoid(up)).astype(BF16)
        out = (resid + dot(hidden, down_ref[...])).astype(BF16)
        teacher_ref[rows, :] = out
        return out

    for o in range(1, members):
        _, other = peer("member", o)
        teacher(pl.multiple_of(other * block, block))
        for c in range(parts):
            sent["teacher", o, c].start()
    t_all[pl.ds(0, block)] = teacher(pl.multiple_of(m * block, block))
    result = pltpu.make_async_copy(teacher_ref, teacher_hbm, load_sem.at[len(pairs)])
    result.start()

    for o in range(1, members):
        sent["state", o].wait_recv()
        sent["noise", o].wait_recv()
        student(o)
    x_turned[...] = x_all[...].T
    n_turned[...] = n_all[...].T
    sh_turned[...] = sh_all[...].T
    sout_turned[...] = sout_ref[...].T
    chunk = 16
    lanes = 256 if width % 256 == 0 else width
    scale = 1.0 / math.sqrt(cells * tiles)
    c_cross = 1.0 / (members * members)
    c_within = 1.0 / (members * (members - 1))

    def visit(i, losses):
        base = pl.multiple_of(i * chunk, chunk)
        rows = [pl.ds(pl.multiple_of(j * block + base, chunk), chunk) for j in range(members)]
        for at in range(0, width, lanes):
            cols = pl.ds(at, lanes)
            st = [s_all[r, cols].astype(F32) for r in rows]
            te = [t_all[r, cols].astype(F32) for r in rows]
            grads = [jnp.zeros((chunk, lanes), F32) for _ in rows]
            cross = jnp.zeros((chunk, lanes), F32)
            within = jnp.zeros((chunk, lanes), F32)
            for a in range(members):
                for b in range(members):
                    d = st[a] - te[b]
                    q = d * d + 0.01
                    inv = lax.rsqrt(q)
                    grads[a] = grads[a] + d * inv
                    cross = cross + (q * inv - 0.1)
            grads = [g * c_cross for g in grads]
            for a in range(members):
                for b in range(a + 1, members):
                    d = st[a] - st[b]
                    q = d * d + 0.01
                    inv = lax.rsqrt(q)
                    slope = d * inv * c_within
                    grads[a] = grads[a] - slope
                    grads[b] = grads[b] + slope
                    within = within + (q * inv - 0.1)
            for r, g in zip(rows, grads):
                g_all[r, cols] = (g * scale).astype(BF16)
            losses = losses + (cross * c_cross - within * c_within)
        return losses

    def backward(c):
        rows = [pl.ds(j * block + c * part_rows, part_rows) for j in range(members)]
        grads = dot(jnp.concatenate([g_all[r, :] for r in rows]), sout_turned[...])
        for j, r in enumerate(rows):
            g = grads[j * part_rows : (j + 1) * part_rows]
            gpre_all[r, :] = (g * slope_all[r, :]).astype(BF16)

    losses = jnp.zeros((chunk, lanes), F32)
    steps = part_rows // chunk
    for c in range(parts):
        for o in range(1, members):
            sent["teacher", o, c].wait_recv()
        losses = lax.fori_loop(c * steps, (c + 1) * steps, visit, losses)
        if c + 1 < parts:
            backward(c)
    total = jnp.sum(losses, keepdims=True)
    lane = lax.broadcasted_iota(jnp.int32, (8, 128), 1)
    onehot = jnp.where(lane == region_ref[...], 1.0, 0.0) * total

    if not reduce_here:
        loss_ref[...] = onehot
        gout_ref[...] = dot(sh_turned[...], g_all[...])
        backward(parts - 1)
        gin_ref[...] = dot(x_turned[...], gpre_all[...])
        gnoise_ref[...] = dot(n_turned[...], gpre_all[...])
        for c in sent.values():
            c.wait_send()
    else:
        bufs = list(bufs)
        loss_bufs = [bufs.pop(0) for _ in streams[0]]
        wire, part, land, share = [], [], [], []
        for order in streams:
            wire.append([bufs.pop(0) for _ in order])
            part.append([bufs.pop(0) for _ in order])
            land.append([bufs.pop(0) for _ in order])
            share.append(bufs.pop(0))
        column = width // members
        loss_now = [onehot]

        def start(s, k):
            step = streams[s][k]
            n = count_of(step, members)
            size = wire[s][k].shape[0] // n
            for o in range(1, n):
                device, other = peer(step, o)
                c = copy(
                    ("grad", s, k, o),
                    wire[s][k].at[pl.ds(other * size, size)],
                    land[s][k].at[o - 1],
                    device,
                )
                c.start()
                sent["grad", s, k, o] = c

        def finish(s, k):
            step = streams[s][k]
            n = count_of(step, members)
            size = wire[s][k].shape[0] // n
            mine = digit_of(step) * size
            for o in range(1, n):
                sent["grad", s, k, o].wait_recv()
            for i in range(size):
                value = part[s][k][mine + i]
                for o in range(1, n):
                    value = value + land[s][k][o - 1, i].astype(F32)
                if k + 1 < len(streams[s]):
                    part[s][k + 1][i] = value
                    wire[s][k + 1][i] = value.astype(BF16)
                else:
                    share[s][m] = value.astype(BF16)

        def start_loss(k):
            step = streams[0][k]
            mine = digit_of(step)
            loss_bufs[k][mine] = loss_now[0]
            for o in range(1, count_of(step, members)):
                device, _ = peer(step, o)
                c = copy(("loss", k, o), loss_bufs[k].at[mine], loss_bufs[k].at[mine], device)
                c.start()
                sent["loss", k, o] = c

        def finish_loss(k):
            n = count_of(streams[0][k], members)
            for o in range(1, n):
                sent["loss", k, o].wait_recv()
            value = loss_bufs[k][0]
            for j in range(1, n):
                value = value + loss_bufs[k][j]
            loss_now[0] = value

        def put(s, acc):
            rows = acc.shape[0] // tiles
            span = column if "member" in streams[s] else width
            for i in range(width // span):
                for j in range(tiles):
                    slot = slot_of(streams[s], members, i, j)
                    value = acc[j * rows : (j + 1) * rows, i * span : (i + 1) * span]
                    if rows % 16:
                        value = jnp.concatenate([value[:, : span // 2], value[:, span // 2 :]])
                    part[s][0][slot] = value
                    wire[s][0][slot] = value.astype(BF16)

        start_loss(0)
        put(0, dot(sh_turned[...], g_all[...]))
        start(0, 0)
        backward(parts - 1)
        put(1, dot(x_turned[...], gpre_all[...]))
        start(1, 0)
        finish(0, 0)
        start(0, 1)
        put(2, dot(n_turned[...], gpre_all[...]))
        start(2, 0)

        def start_share(s):
            for o in range(1, members):
                device, _ = peer("member", o)
                c = copy(("share", s, o), share[s].at[m], share[s].at[m], device)
                c.start()
                sent["share", s, o] = c

        for k in range(len(streams[0])):
            finish_loss(k)
            if k + 1 < len(streams[0]):
                start_loss(k + 1)
            for s in range(len(streams)):
                if k < len(streams[s]):
                    if (s, k) != (0, 0):
                        finish(s, k)
                        if k + 1 < len(streams[s]):
                            start(s, k + 1)
                        else:
                            start_share(s)
        loss_ref[...] = loss_now[0] * (1.0 / (cells * tiles // REGIONS * width))
        for s in (1, 2, 0):
            for o in range(1, members):
                sent["share", s, o].wait_recv()
            pieces = [share[s][j].astype(F32) for j in range(members)]
            if s == 0:
                for j in range(members):
                    gout_ref[:, j * column : (j + 1) * column] = pieces[j]
            else:
                total = sum(pieces[1:], pieces[0])
                if s == 1:
                    gin_ref[...] = total
                else:
                    rows = gnoise_ref.shape[0]
                    if rows % 16:
                        total = jnp.concatenate([total[:rows], total[rows:]], axis=1)
                    gnoise_ref[...] = total
        for c in sent.values():
            c.wait_send()

    result.wait()

    @pl.when(t > 0)
    def _():
        to_left.wait_send()

    @pl.when(t < tiles - 1)
    def _():
        to_right.wait_send()


def hand_on(*refs):
    for i in range(4):
        refs[5 + i][...] = refs[i][...]
    refs[9][...] = refs[4][0, : refs[9].shape[0]]


def on_device(members, tiles, *args):
    state, noise, neighbours, region_map = args[0][0], args[1][0], args[2], args[3]
    weights = args[4:]
    cells, width = state.shape
    draws = noise.shape[1]
    hidden = weights[3].shape[1]
    rows = [hidden // tiles, width // tiles, draws // tiles]
    column = width // members
    reduce_here = (
        rows[0] % 16 == 0
        and rows[1] % 16 == 0
        and rows[2] % 8 == 0
        and column % 128 == 0
        and hidden == width
        and tiles >= 8
        and members > 1
    )
    scratch = [
        pltpu.VMEM((cells + 2 * HALO, width), BF16),
        pltpu.VMEM((cells, width), BF16),
        pltpu.VMEM((cells, width), BF16),
        pltpu.VMEM((cells, draws), BF16),
        pltpu.VMEM((cells, width), BF16),
        pltpu.VMEM((cells, width), BF16),
        pltpu.VMEM((cells, hidden), F32),
        pltpu.VMEM((cells, hidden), BF16),
        pltpu.VMEM((cells, width), BF16),
        pltpu.VMEM((cells, hidden), BF16),
        pltpu.VMEM((width, cells), BF16),
        pltpu.VMEM((draws, cells), BF16),
        pltpu.VMEM((hidden, cells), BF16),
        pltpu.VMEM((width, hidden), BF16),
        pltpu.VMEM((cells, width), BF16),
        pltpu.VMEM(neighbours.shape, neighbours.dtype),
        pltpu.VMEM((1, 1), region_map.dtype),
    ]
    scratch += [pltpu.VMEM(w.shape, w.dtype) for w in weights]
    copies = len(layout(members, tiles, parts_of(cells // members)))
    scratch += [pltpu.SemaphoreType.DMA((n,)) for n in (len(weights) + 6, copies, copies)]
    if reduce_here:
        shapes = ((rows[1], width), (rows[2], width), (rows[0], width))
        streams = orders(tiles)
        for step in streams[0]:
            scratch.append(pltpu.VMEM((count_of(step, members), 8, 128), F32))
        noise_piece = (2 * rows[2], width // 2) if rows[2] % 16 else (rows[2], width)
        pieces = [(rows[0], column), (rows[1], width), noise_piece]
        for order, piece in zip(streams, pieces):
            sizes = []
            left = (members if "member" in order else 1) * tiles
            for step in order:
                sizes.append((left, count_of(step, members)))
                left //= count_of(step, members)
            scratch += [pltpu.VMEM((size,) + piece, BF16) for size, _ in sizes]
            scratch += [pltpu.VMEM((size,) + piece, F32) for size, _ in sizes]
            scratch += [pltpu.VMEM((n - 1, size // n) + piece, BF16) for size, n in sizes]
            scratch.append(pltpu.VMEM((members,) + piece, BF16))
    else:
        shapes = ((width, hidden), (draws, hidden), (hidden, width))
    vmem = pl.BlockSpec(memory_space=pltpu.VMEM)
    teacher, loss, gin, gnoise, gout = pl.pallas_call(
        functools.partial(kernel, members, tiles, reduce_here),
        out_shape=[jax.ShapeDtypeStruct((cells, width), BF16), jax.ShapeDtypeStruct((8, 128), F32)]
        + [jax.ShapeDtypeStruct(s, F32) for s in shapes],
        in_specs=[pl.BlockSpec(memory_space=pl.ANY)] * 10,
        out_specs=[pl.BlockSpec(memory_space=pl.ANY)] + [vmem] * 4,
        scratch_shapes=scratch,
        compiler_params=pltpu.CompilerParams(
            collective_id=0, has_side_effects=True, vmem_limit_bytes=56 * 1024 * 1024
        ),
    )(state, noise, neighbours, region_map.reshape(1, 1), *weights)
    if reduce_here:
        big = (teacher, gin, gnoise, gout)
        teacher, gin, gnoise, gout, region_loss = pl.pallas_call(
            hand_on,
            out_shape=[jax.ShapeDtypeStruct(a.shape, a.dtype) for a in big]
            + [jax.ShapeDtypeStruct((REGIONS,), F32)],
            in_specs=[vmem] * 5,
            out_specs=[vmem] * 5,
        )(*big, loss)
    else:
        region_loss = loss[0, :REGIONS]
        region_loss = lax.psum(region_loss, ("member", "tile")) / (cells * tiles // REGIONS * width)
        gin, gnoise, gout = lax.psum(
            tuple(
                lax.psum_scatter(g, "tile", scatter_dimension=0, tiled=True)
                for g in (gin, gnoise, gout)
            ),
            "member",
        )
    return teacher[None], region_loss, gin, gnoise, gout


def solution(mesh):
    in_specs = (
        P("member", "tile", None),
        P("member", "tile", None),
        P(None, "tile"),
        P("tile"),
        P(),
        P(),
        P(),
        P(),
        P(),
        P(),
    )
    out_specs = (P("member", "tile", None), P(), P("tile", None), P("tile", None), P("tile", None))
    return jax.shard_map(
        functools.partial(on_device, mesh.shape["member"], mesh.shape["tile"]),
        mesh=mesh,
        in_specs=in_specs,
        out_specs=out_specs,
        check_vma=False,
    )
```

```python
import functools
import math

import jax
import jax.numpy as jnp
from jax import lax
from jax.experimental import pallas as pl
from jax.experimental.pallas import tpu as pltpu
from jax.sharding import PartitionSpec as P

HALO = 64
REGIONS = 8
MESH = pl.DeviceIdType.MESH
F32 = jnp.float32
BF16 = jnp.bfloat16


def dot(a, b):
    return jnp.dot(a, b, preferred_element_type=F32)


def dot_tn(a, b):
    return lax.dot_general(a, b, (((0,), (0,)), ((), ())), preferred_element_type=F32)


def tile_digits(tiles):
    digits = []
    stride = 1
    for _ in range(2):
        if tiles // stride % 2 == 0 and tiles // stride > 2:
            digits.append((stride, 2))
            stride *= 2
    digits.append((stride, tiles // stride))
    return digits


def orders(tiles):
    digits = tile_digits(tiles)
    first = [digits[0], "member"] + digits[1:]
    second = digits
    third = digits[:1] + digits[2:] + digits[1:2]
    return first, second, third


def count_of(step, members):
    return members if step == "member" else step[1]


def slot_of(order, members, member, tile):
    slot = 0
    for step in order:
        n = count_of(step, members)
        slot = slot * n + (member if step == "member" else tile // step[0] % n)
    return slot


def parts_of(block):
    return 4 if block % 64 == 0 else 1


def layout(members, tiles, parts):
    names = ["left", "right"]
    for o in range(1, members):
        names += [("state", o), ("noise", o)] + [("teacher", o, c) for c in range(parts)]
    for s, order in enumerate(orders(tiles)):
        for k, step in enumerate(order):
            for o in range(1, count_of(step, members)):
                names.append(("grad", s, k, o))
                if s == 0:
                    names.append(("loss", k, o))
        for o in range(1, members):
            names.append(("share", s, o))
    return {name: i for i, name in enumerate(names)}


def kernel(
    members,
    tiles,
    reduce_here,
    state_hbm,
    noise_hbm,
    neigh_hbm,
    region_hbm,
    msg_hbm,
    up_hbm,
    down_hbm,
    sin_hbm,
    snoise_hbm,
    sout_hbm,
    teacher_hbm,
    loss_ref,
    gin_ref,
    gnoise_ref,
    gout_ref,
    ext,
    gathered,
    x_all,
    n_all,
    t_all,
    s_all,
    slope_all,
    sh_all,
    g_all,
    gpre_all,
    x_turned,
    n_turned,
    sh_turned,
    sout_turned,
    teacher_ref,
    neigh_ref,
    region_ref,
    msg_ref,
    up_ref,
    down_ref,
    sin_ref,
    snoise_ref,
    sout_ref,
    load_sem,
    send_sem,
    recv_sem,
    *bufs,
):
    cells, width = state_hbm.shape
    block = cells // members
    m = lax.axis_index("member")
    t = lax.axis_index("tile")
    parts = parts_of(block)
    part_rows = block // parts
    ids = layout(members, tiles, parts)
    streams = orders(tiles)

    def peer(step, o):
        if step == "member":
            other = lax.rem(m + o, members)
            return (other, t), other
        stride, n = step
        digit = lax.rem(t // stride, n)
        other = lax.rem(digit + o, n)
        return (m, t + (other - digit) * stride), other

    def digit_of(step):
        return m if step == "member" else lax.rem(t // step[0], step[1])

    def copy(name, src, dst, device):
        i = ids[name]
        return pltpu.make_async_remote_copy(
            src_ref=src,
            dst_ref=dst,
            send_sem=send_sem.at[i],
            recv_sem=recv_sem.at[i],
            device_id=device,
            device_id_type=MESH,
        )

    own = pl.ds(pl.multiple_of(m * block, block), block)
    pairs = [
        (state_hbm.at[own], x_all.at[pl.ds(0, block)]),
        (noise_hbm.at[own], n_all.at[pl.ds(0, block)]),
        (sin_hbm, sin_ref),
        (snoise_hbm, snoise_ref),
        (sout_hbm, sout_ref),
        (state_hbm, ext.at[pl.ds(HALO, cells)]),
        (neigh_hbm, neigh_ref),
        (msg_hbm, msg_ref),
        (up_hbm, up_ref),
        (down_hbm, down_ref),
        (region_hbm, region_ref),
    ]
    barrier = pltpu.get_barrier_semaphore()
    groups = ["member"] + (tile_digits(tiles) if reduce_here else [])
    waits = 0
    for step in groups:
        for o in range(1, count_of(step, members)):
            device, _ = peer(step, o)
            pl.semaphore_signal(barrier, inc=1, device_id=device, device_id_type=MESH)
            waits += 1

    @pl.when(t > 0)
    def _():
        pl.semaphore_signal(barrier, inc=1, device_id=(m, t - 1), device_id_type=MESH)

    @pl.when(t < tiles - 1)
    def _():
        pl.semaphore_signal(barrier, inc=1, device_id=(m, t + 1), device_id_type=MESH)

    loads = [pltpu.make_async_copy(a, b, load_sem.at[i]) for i, (a, b) in enumerate(pairs)]
    for load in loads:
        load.start()
    ends = jnp.where(t > 0, 1, 0) + jnp.where(t < tiles - 1, 1, 0)
    pl.semaphore_wait(barrier, waits + ends)

    to_left = copy("left", state_hbm.at[pl.ds(0, HALO)], ext.at[pl.ds(HALO + cells, HALO)], (m, t - 1))
    to_right = copy("right", state_hbm.at[pl.ds(cells - HALO, HALO)], ext.at[pl.ds(0, HALO)], (m, t + 1))

    @pl.when(t > 0)
    def _():
        to_left.start()

    @pl.when(t < tiles - 1)
    def _():
        to_right.start()

    pending = []
    sent = {}
    for o in range(1, members):
        device, other = peer("member", o)
        rows = pl.ds(pl.multiple_of(other * block, block), block)
        slot = pl.ds(o * block, block)
        sent["state", o] = copy(("state", o), state_hbm.at[rows], x_all.at[slot], device)
        sent["noise", o] = copy(("noise", o), noise_hbm.at[rows], n_all.at[slot], device)
        sent["state", o].start()
        sent["noise", o].start()
        for c in range(parts):
            rows = pl.ds(pl.multiple_of(other * block + c * part_rows, part_rows), part_rows)
            slot = pl.ds(o * block + c * part_rows, part_rows)
            name = ("teacher", o, c)
            sent[name] = copy(name, teacher_ref.at[rows], t_all.at[slot], device)

    def student(o):
        rows = pl.ds(o * block, block)
        x = x_all[rows, :]
        pre = dot(x, sin_ref[...]) + dot(n_all[rows, :], snoise_ref[...])
        sig = jax.nn.sigmoid(pre)
        slope_all[rows, :] = sig * (1.0 + pre * (1.0 - sig))
        sh = (pre * sig).astype(BF16)
        sh_all[rows, :] = sh
        s_all[rows, :] = (x.astype(F32) + dot(sh, sout_ref[...])).astype(BF16)

    for load in loads[:5]:
        load.wait()
    student(0)

    zeros = jnp.zeros((HALO, width), BF16)

    @pl.when(t > 0)
    def _():
        to_right.wait_recv()

    @pl.when(t == 0)
    def _():
        ext[pl.ds(0, HALO)] = zeros

    @pl.when(t < tiles - 1)
    def _():
        to_left.wait_recv()

    @pl.when(t == tiles - 1)
    def _():
        ext[pl.ds(HALO + cells, HALO)] = zeros

    for load in loads[5:]:
        load.wait()

    span = 128
    reach = span + 2 * HALO
    nbrs = neigh_ref.shape[0]
    for b in range(cells // span):
        lines = lax.broadcasted_iota(jnp.int32, (reach, span), 0) + b * span
        times = jnp.zeros((reach, span), F32)
        for k in range(nbrs):
            index = neigh_ref[pl.ds(k, 1), pl.ds(b * span, span)]
            times = times + jnp.where(lines == index, 1.0, 0.0)
        total = dot_tn(times.astype(BF16), ext[pl.ds(b * span, reach), :])
        gathered[pl.ds(b * span, span)] = (total / nbrs).astype(BF16)

    def teacher(at):
        rows = pl.ds(at, block)
        resid = ext[pl.ds(at + HALO, block), :].astype(F32) + dot(gathered[rows, :], msg_ref[...])
        mean = jnp.mean(resid * resid, axis=1, keepdims=True)
        normed = (resid * lax.rsqrt(mean + 1e-06)).astype(BF16)
        up = dot(normed, up_ref[...])
        hidden = (up * jax.nn.sigmoid(up)).astype(BF16)
        out = (resid + dot(hidden, down_ref[...])).astype(BF16)
        teacher_ref[rows, :] = out
        return out

    for o in range(1, members):
        _, other = peer("member", o)
        teacher(pl.multiple_of(other * block, block))
        for c in range(parts):
            sent["teacher", o, c].start()
    t_all[pl.ds(0, block)] = teacher(pl.multiple_of(m * block, block))
    result = pltpu.make_async_copy(teacher_ref, teacher_hbm, load_sem.at[len(pairs)])
    result.start()

    for o in range(1, members):
        sent["state", o].wait_recv()
        sent["noise", o].wait_recv()
        student(o)
    x_turned[...] = x_all[...].T
    n_turned[...] = n_all[...].T
    sh_turned[...] = sh_all[...].T
    sout_turned[...] = sout_ref[...].T
    chunk = 16
    lanes = 256 if width % 256 == 0 else width
    scale = 1.0 / math.sqrt(cells * tiles)
    c_cross = 1.0 / (members * members)
    c_within = 1.0 / (members * (members - 1))

    def visit(i, losses):
        base = pl.multiple_of(i * chunk, chunk)
        rows = [pl.ds(pl.multiple_of(j * block + base, chunk), chunk) for j in range(members)]
        for at in range(0, width, lanes):
            cols = pl.ds(at, lanes)
            st = [s_all[r, cols].astype(F32) for r in rows]
            te = [t_all[r, cols].astype(F32) for r in rows]
            grads = [jnp.zeros((chunk, lanes), F32) for _ in rows]
            cross = jnp.zeros((chunk, lanes), F32)
            within = jnp.zeros((chunk, lanes), F32)
            for a in range(members):
                for b in range(members):
                    d = st[a] - te[b]
                    q = d * d + 0.01
                    inv = lax.rsqrt(q)
                    grads[a] = grads[a] + d * inv
                    cross = cross + (q * inv - 0.1)
            grads = [g * c_cross for g in grads]
            for a in range(members):
                for b in range(a + 1, members):
                    d = st[a] - st[b]
                    q = d * d + 0.01
                    inv = lax.rsqrt(q)
                    slope = d * inv * c_within
                    grads[a] = grads[a] - slope
                    grads[b] = grads[b] + slope
                    within = within + (q * inv - 0.1)
            for r, g in zip(rows, grads):
                g_all[r, cols] = (g * scale).astype(BF16)
            losses = losses + (cross * c_cross - within * c_within)
        return losses

    def backward(c):
        rows = [pl.ds(j * block + c * part_rows, part_rows) for j in range(members)]
        grads = dot(jnp.concatenate([g_all[r, :] for r in rows]), sout_turned[...])
        for j, r in enumerate(rows):
            g = grads[j * part_rows : (j + 1) * part_rows]
            gpre_all[r, :] = (g * slope_all[r, :]).astype(BF16)

    losses = jnp.zeros((chunk, lanes), F32)
    steps = part_rows // chunk
    for c in range(parts):
        for o in range(1, members):
            sent["teacher", o, c].wait_recv()
        losses = lax.fori_loop(c * steps, (c + 1) * steps, visit, losses)
        if c + 1 < parts:
            backward(c)
    total = jnp.sum(losses, keepdims=True)
    lane = lax.broadcasted_iota(jnp.int32, (8, 128), 1)
    onehot = jnp.where(lane == region_ref[...], 1.0, 0.0) * total

    if not reduce_here:
        loss_ref[...] = onehot
        gout_ref[...] = dot(sh_turned[...], g_all[...])
        backward(parts - 1)
        gin_ref[...] = dot(x_turned[...], gpre_all[...])
        gnoise_ref[...] = dot(n_turned[...], gpre_all[...])
        for c in sent.values():
            c.wait_send()
    else:
        bufs = list(bufs)
        loss_bufs = [bufs.pop(0) for _ in streams[0]]
        wire, part, land, share = [], [], [], []
        for order in streams:
            wire.append([bufs.pop(0) for _ in order])
            part.append([bufs.pop(0) for _ in order])
            land.append([bufs.pop(0) for _ in order])
            share.append(bufs.pop(0))
        column = width // members
        loss_now = [onehot]

        def start(s, k):
            step = streams[s][k]
            n = count_of(step, members)
            size = wire[s][k].shape[0] // n
            for o in range(1, n):
                device, other = peer(step, o)
                c = copy(
                    ("grad", s, k, o),
                    wire[s][k].at[pl.ds(other * size, size)],
                    land[s][k].at[o - 1],
                    device,
                )
                c.start()
                sent["grad", s, k, o] = c

        def finish(s, k):
            step = streams[s][k]
            n = count_of(step, members)
            size = wire[s][k].shape[0] // n
            mine = digit_of(step) * size
            for o in range(1, n):
                sent["grad", s, k, o].wait_recv()
            for i in range(size):
                value = part[s][k][mine + i]
                for o in range(1, n):
                    value = value + land[s][k][o - 1, i].astype(F32)
                if k + 1 < len(streams[s]):
                    part[s][k + 1][i] = value
                    wire[s][k + 1][i] = value.astype(BF16)
                else:
                    share[s][m] = value.astype(BF16)

        def start_loss(k):
            step = streams[0][k]
            mine = digit_of(step)
            loss_bufs[k][mine] = loss_now[0]
            for o in range(1, count_of(step, members)):
                device, _ = peer(step, o)
                c = copy(("loss", k, o), loss_bufs[k].at[mine], loss_bufs[k].at[mine], device)
                c.start()
                sent["loss", k, o] = c

        def finish_loss(k):
            n = count_of(streams[0][k], members)
            for o in range(1, n):
                sent["loss", k, o].wait_recv()
            value = loss_bufs[k][0]
            for j in range(1, n):
                value = value + loss_bufs[k][j]
            loss_now[0] = value

        def put(s, acc):
            rows = acc.shape[0] // tiles
            span = column if "member" in streams[s] else width
            for i in range(width // span):
                for j in range(tiles):
                    slot = slot_of(streams[s], members, i, j)
                    value = acc[j * rows : (j + 1) * rows, i * span : (i + 1) * span]
                    if rows % 16:
                        value = jnp.concatenate([value[:, : span // 2], value[:, span // 2 :]])
                    part[s][0][slot] = value
                    wire[s][0][slot] = value.astype(BF16)

        start_loss(0)
        put(0, dot(sh_turned[...], g_all[...]))
        start(0, 0)
        backward(parts - 1)
        acc_in = dot(x_turned[...], gpre_all[...])
        finish(0, 0)
        start(0, 1)
        put(1, acc_in)
        start(1, 0)
        put(2, dot(n_turned[...], gpre_all[...]))
        start(2, 0)

        def start_share(s):
            for o in range(1, members):
                device, _ = peer("member", o)
                c = copy(("share", s, o), share[s].at[m], share[s].at[m], device)
                c.start()
                sent["share", s, o] = c

        for k in range(len(streams[0])):
            finish_loss(k)
            if k + 1 < len(streams[0]):
                start_loss(k + 1)
            for s in range(len(streams)):
                if k < len(streams[s]):
                    if (s, k) != (0, 0):
                        finish(s, k)
                        if k + 1 < len(streams[s]):
                            start(s, k + 1)
                        else:
                            start_share(s)
        loss_ref[...] = loss_now[0] * (1.0 / (cells * tiles // REGIONS * width))
        for s in (1, 2, 0):
            for o in range(1, members):
                sent["share", s, o].wait_recv()
            pieces = [share[s][j].astype(F32) for j in range(members)]
            if s == 0:
                for j in range(members):
                    gout_ref[:, j * column : (j + 1) * column] = pieces[j]
            else:
                total = sum(pieces[1:], pieces[0])
                if s == 1:
                    gin_ref[...] = total
                else:
                    rows = gnoise_ref.shape[0]
                    if rows % 16:
                        total = jnp.concatenate([total[:rows], total[rows:]], axis=1)
                    gnoise_ref[...] = total
        for c in sent.values():
            c.wait_send()

    result.wait()

    @pl.when(t > 0)
    def _():
        to_left.wait_send()

    @pl.when(t < tiles - 1)
    def _():
        to_right.wait_send()


def hand_on(*refs):
    for i in range(4):
        refs[5 + i][...] = refs[i][...]
    refs[9][...] = refs[4][0, : refs[9].shape[0]]


def on_device(members, tiles, *args):
    state, noise, neighbours, region_map = args[0][0], args[1][0], args[2], args[3]
    weights = args[4:]
    cells, width = state.shape
    draws = noise.shape[1]
    hidden = weights[3].shape[1]
    rows = [hidden // tiles, width // tiles, draws // tiles]
    column = width // members
    reduce_here = (
        rows[0] % 16 == 0
        and rows[1] % 16 == 0
        and rows[2] % 8 == 0
        and column % 128 == 0
        and hidden == width
        and tiles >= 8
        and members > 1
    )
    scratch = [
        pltpu.VMEM((cells + 2 * HALO, width), BF16),
        pltpu.VMEM((cells, width), BF16),
        pltpu.VMEM((cells, width), BF16),
        pltpu.VMEM((cells, draws), BF16),
        pltpu.VMEM((cells, width), BF16),
        pltpu.VMEM((cells, width), BF16),
        pltpu.VMEM((cells, hidden), F32),
        pltpu.VMEM((cells, hidden), BF16),
        pltpu.VMEM((cells, width), BF16),
        pltpu.VMEM((cells, hidden), BF16),
        pltpu.VMEM((width, cells), BF16),
        pltpu.VMEM((draws, cells), BF16),
        pltpu.VMEM((hidden, cells), BF16),
        pltpu.VMEM((width, hidden), BF16),
        pltpu.VMEM((cells, width), BF16),
        pltpu.VMEM(neighbours.shape, neighbours.dtype),
        pltpu.VMEM((1, 1), region_map.dtype),
    ]
    scratch += [pltpu.VMEM(w.shape, w.dtype) for w in weights]
    copies = len(layout(members, tiles, parts_of(cells // members)))
    scratch += [pltpu.SemaphoreType.DMA((n,)) for n in (len(weights) + 6, copies, copies)]
    if reduce_here:
        shapes = ((rows[1], width), (rows[2], width), (rows[0], width))
        streams = orders(tiles)
        for step in streams[0]:
            scratch.append(pltpu.VMEM((count_of(step, members), 8, 128), F32))
        noise_piece = (2 * rows[2], width // 2) if rows[2] % 16 else (rows[2], width)
        pieces = [(rows[0], column), (rows[1], width), noise_piece]
        for order, piece in zip(streams, pieces):
            sizes = []
            left = (members if "member" in order else 1) * tiles
            for step in order:
                sizes.append((left, count_of(step, members)))
                left //= count_of(step, members)
            scratch += [pltpu.VMEM((size,) + piece, BF16) for size, _ in sizes]
            scratch += [pltpu.VMEM((size,) + piece, F32) for size, _ in sizes]
            scratch += [pltpu.VMEM((n - 1, size // n) + piece, BF16) for size, n in sizes]
            scratch.append(pltpu.VMEM((members,) + piece, BF16))
    else:
        shapes = ((width, hidden), (draws, hidden), (hidden, width))
    vmem = pl.BlockSpec(memory_space=pltpu.VMEM)
    teacher, loss, gin, gnoise, gout = pl.pallas_call(
        functools.partial(kernel, members, tiles, reduce_here),
        out_shape=[jax.ShapeDtypeStruct((cells, width), BF16), jax.ShapeDtypeStruct((8, 128), F32)]
        + [jax.ShapeDtypeStruct(s, F32) for s in shapes],
        in_specs=[pl.BlockSpec(memory_space=pl.ANY)] * 10,
        out_specs=[pl.BlockSpec(memory_space=pl.ANY)] + [vmem] * 4,
        scratch_shapes=scratch,
        compiler_params=pltpu.CompilerParams(
            collective_id=0, has_side_effects=True, vmem_limit_bytes=56 * 1024 * 1024
        ),
    )(state, noise, neighbours, region_map.reshape(1, 1), *weights)
    if reduce_here:
        big = (teacher, gin, gnoise, gout)
        teacher, gin, gnoise, gout, region_loss = pl.pallas_call(
            hand_on,
            out_shape=[jax.ShapeDtypeStruct(a.shape, a.dtype) for a in big]
            + [jax.ShapeDtypeStruct((REGIONS,), F32)],
            in_specs=[vmem] * 5,
            out_specs=[vmem] * 5,
        )(*big, loss)
    else:
        region_loss = loss[0, :REGIONS]
        region_loss = lax.psum(region_loss, ("member", "tile")) / (cells * tiles // REGIONS * width)
        gin, gnoise, gout = lax.psum(
            tuple(
                lax.psum_scatter(g, "tile", scatter_dimension=0, tiled=True)
                for g in (gin, gnoise, gout)
            ),
            "member",
        )
    return teacher[None], region_loss, gin, gnoise, gout


def solution(mesh):
    in_specs = (
        P("member", "tile", None),
        P("member", "tile", None),
        P(None, "tile"),
        P("tile"),
        P(),
        P(),
        P(),
        P(),
        P(),
        P(),
    )
    out_specs = (P("member", "tile", None), P(), P("tile", None), P("tile", None), P("tile", None))
    return jax.shard_map(
        functools.partial(on_device, mesh.shape["member"], mesh.shape["tile"]),
        mesh=mesh,
        in_specs=in_specs,
        out_specs=out_specs,
        check_vma=False,
    )
```
